32 devices in a mesh: lat: 4 (over y, core), lon: 8 (over z, x).
Axes of the slice: x: 2, y: 2, z: 4, core: 2. Of those that a mesh axis runs over, the one named last changes fastest.
Arguments:
- grid_fields: bfloat16 [24, 64, 1024], P(None, 'lat', 'lon'), may hold values from -6 to 6
- obs_values: bfloat16 [32, 32, 16, 128], P(('lat', 'lon')), may hold values from -6 to 6
- obs_count: int32 [32, 32], P(('lat', 'lon')), may hold values from 0 to 16, as said below
- obs_cell: int32 [32, 32, 16], P(('lat', 'lon')), may hold values from 0 to 2047
- obs_valid: int32 [32, 32, 16], P(('lat', 'lon')), may hold values 0 or 1
- obs_dist2: float32 [32, 32, 16], P(('lat', 'lon')), may hold values from 0.01 to 4
- field_weight: bfloat16 [24, 128], replicated, may hold values from -1.25 to 1.25
- obs_weight: bfloat16 [128, 128], replicated, may hold values from -0.5 to 0.5
- conv_kernel: bfloat16 [2, 5, 5, 128, 128], replicated, may hold values from -0.109375 to 0.109375
- cotangent: bfloat16 [64, 1024, 128], P('lat', 'lon'), may hold values from -6 to 6
Outputs:
- encoded: bfloat16 [64, 1024, 128], P('lat', 'lon')
- kernel_grad: float32 [2, 5, 5, 128, 128], replicated
- obs_weight_grad: float32 [128, 128], replicated
- field_weight_grad: float32 [24, 128], replicated
The draws below stay inside these ranges and needn't reach their ends.
Inputs may be any that keep to these rules, and one draw needn't show every extreme that they name: Rows from slot index obs_count onwards are padding. Every tile receives a full slot of 16 rows from some sending device.
All inputs are finite; a program needn't handle non-finite values. No bound on the sum of `obs_valid` on one device may be relied on, other than what follows from the above.
Results may differ from the reference program's by a relative error of at most 0.01.
Values may be sent and summed in bfloat16 or wider, within the bound.
A program may use at most 128 MiB of HBM per device.

```python
import math
import jax
import jax.numpy as jnp

LAT_DEV = 16
LON_DEV = 128
CH = 128
VALS = 128
FIELDS = 24
CAP = 16
TILES = 32
LAT_ALL = 64
LON_ALL = 1024
N_LAT = 4
N_LON = 8


def draw_obs_count(key, part):
    first, second, third = jax.random.split(key, 3)
    density = jax.random.randint(first, (TILES,), 1, 9)
    raw_count = jax.random.randint(second, (TILES, TILES), 0, CAP + 1)
    counted = jnp.minimum(CAP, raw_count * density[None, :] // 4)
    filler = jax.random.randint(third, (TILES,), 0, TILES)
    senders = jnp.arange(TILES, dtype=jnp.int32)[:, None]
    return jnp.where(senders == filler[None, :], CAP, counted).astype(jnp.int32)


def plant(result, key, smallest, top_value):
    place = [jax.random.randint(jax.random.fold_in(key, axis), (), 0, length) for axis, length in enumerate(result.shape)]
    longest = result.shape.index(max(result.shape))
    next_to = place[:longest] + [(place[longest] + 1) % result.shape[longest]] + place[longest + 1:]
    return result.at[tuple(place)].set(smallest).at[tuple(next_to)].set(top_value)


def level_of(stream_key, extent, cuts, smallest, largest):
    level = 1.0
    for axis_at, parts in cuts:
        heights = jax.random.uniform(jax.random.fold_in(jax.random.fold_in(stream_key, 6), axis_at), (parts,), jnp.float32, smallest / len(cuts), largest / len(cuts))
        level = level * jnp.repeat(jnp.exp(heights), extent[axis_at] // parts).reshape((-1,) + (1,) * (len(extent) - 1 - axis_at))
    return level


def scatter_about(key, dims, spread, reach, cuts=(), kind=jnp.bfloat16):
    level = level_of(key, dims, cuts, -0.22, 0.18) if cuts else 1.0
    result = jax.random.normal(key, dims, jnp.float32) * spread * level
    return jnp.minimum(jnp.maximum(result, -reach), reach).astype(kind)


def setup_inputs(seed: int = 0) -> dict:
    keys = jax.random.split(jax.random.key(seed), 11)
    return {
        "grid_fields": scatter_about(keys[0], (FIELDS, LAT_ALL, LON_ALL), 1.0, 6.0, ((1, 4), (2, 8))),
        "obs_values": scatter_about(keys[1], (TILES, TILES, CAP, VALS), 1.0, 6.0, ((0, 32),)),
        "obs_count": draw_obs_count(jax.random.fold_in(keys[10], 71), 0),
        "obs_cell": plant(jax.random.randint(keys[3], (TILES, TILES, CAP), 0, LAT_DEV * LON_DEV), jax.random.fold_in(keys[3], 1), 0, (LAT_DEV * LON_DEV) - 1).astype(jnp.int32),
        "obs_valid": plant((jax.random.randint(keys[4], (TILES, TILES, CAP), 0, 8) < 7).astype(jnp.int32), jax.random.fold_in(keys[4], 1), 0, 1),
        "obs_dist2": jnp.clip(jnp.exp(math.log(4.0) - 5.9914646 * jax.random.uniform(keys[5], (TILES, TILES, CAP), jnp.float32) ** level_of(keys[5], (TILES, TILES, CAP), ((0, 32),), -0.2, 0.2)), 0.01, 4.0),
        "field_weight": scatter_about(keys[6], (FIELDS, CH), FIELDS ** -0.5, 1.25),
        "obs_weight": scatter_about(keys[7], (VALS, CH), VALS ** -0.5, 0.5),
        "conv_kernel": scatter_about(keys[8], (2, 5, 5, CH, CH), (25 * CH) ** -0.5, 0.109375),
        "cotangent": scatter_about(keys[9], (LAT_ALL, LON_ALL, CH), 1.0, 6.0, ((0, 4), (1, 8))),
    }


def extend(field):
    wrapped = jnp.concatenate([field[:, -2:], field, field[:, :2]], axis=1)
    return jnp.pad(wrapped, ((2, 2), (0, 0), (0, 0)))

def forward_conv(padded, kernel, lat_rows, lon_cols):
    channels = kernel.shape[-1]
    summed = jnp.zeros((lat_rows * lon_cols, channels), jnp.float32)
    for row_tap in range(5):
        for col_tap in range(5):
            window = padded[row_tap:row_tap + lat_rows, col_tap:col_tap + lon_cols].reshape(-1, channels)
            summed = summed + jnp.dot(window, kernel[row_tap, col_tap], preferred_element_type=jnp.float32)
    return summed.reshape(lat_rows, lon_cols, channels)

def transpose_conv(padded_grad, kernel, lat_rows, lon_cols):
    channels = kernel.shape[-1]
    summed = jnp.zeros((lat_rows * lon_cols, channels), jnp.float32)
    for row_tap in range(5):
        for col_tap in range(5):
            window = padded_grad[4 - row_tap:4 - row_tap + lat_rows, 4 - col_tap:4 - col_tap + lon_cols].reshape(-1, channels)
            summed = summed + jnp.dot(window, kernel[row_tap, col_tap].T, preferred_element_type=jnp.float32)
    return summed.reshape(lat_rows, lon_cols, channels)

def kernel_terms(padded, grad, lat_rows, lon_cols):
    channels = grad.shape[-1]
    flat_grad = grad.reshape(-1, channels)
    pieces = []
    for row_tap in range(5):
        for col_tap in range(5):
            window = padded[row_tap:row_tap + lat_rows, col_tap:col_tap + lon_cols].reshape(-1, channels)
            pieces.append(jnp.dot(window.T, flat_grad, preferred_element_type=jnp.float32))
    return jnp.stack(pieces).reshape(5, 5, channels, channels)

def gelu_back(inputs, grad):
    _, pullback = jax.vjp(jax.nn.gelu, inputs)
    return pullback(grad)[0]

def reference(grid_fields, obs_values, obs_count, obs_cell, obs_valid, obs_dist2, field_weight, obs_weight, conv_kernel, cotangent):
    lat_rows = LAT_DEV * N_LAT
    lon_cols = LON_DEV * N_LON
    tiles = N_LAT * N_LON
    slots = jnp.arange(CAP, dtype=jnp.int32)
    used = (obs_valid == 1) & (slots[None, None, :] < obs_count[:, :, None])
    obs_w = jnp.where(used, jnp.exp(-0.5 * obs_dist2), 0.0).astype(jnp.bfloat16).astype(jnp.float32)
    target = jnp.arange(tiles, dtype=jnp.int32)[None, :, None]
    grid_row = target // N_LON * LAT_DEV + obs_cell // LON_DEV
    grid_col = target % N_LON * LON_DEV + obs_cell % LON_DEV
    flat_ids = (grid_row * lon_cols + grid_col).reshape(-1).astype(jnp.int32)
    flat_w = obs_w.reshape(-1)
    sums = jax.ops.segment_sum(flat_w[:, None] * obs_values.reshape(-1, VALS).astype(jnp.float32), flat_ids, num_segments=lat_rows * lon_cols)
    dens = jax.ops.segment_sum(flat_w, flat_ids, num_segments=lat_rows * lon_cols)
    feat = (sums / (1.0 + dens)[:, None]).astype(jnp.bfloat16)
    from_fields = jnp.einsum('fhw,fc->hwc', grid_fields.astype(jnp.float32), field_weight.astype(jnp.float32))
    from_obs = jnp.dot(feat, obs_weight, preferred_element_type=jnp.float32).reshape(lat_rows, lon_cols, CH)
    states = [(from_fields + from_obs).astype(jnp.bfloat16)]
    padded_acts = []
    for layer in range(2):
        active = jax.nn.gelu(states[-1].astype(jnp.float32)).astype(jnp.bfloat16)
        padded = extend(active)
        padded_acts.append(padded)
        conv = forward_conv(padded, conv_kernel[layer], lat_rows, lon_cols)
        states.append((states[-1].astype(jnp.float32) + conv).astype(jnp.bfloat16))
    grad = cotangent
    kernel_parts = [None, None]
    for layer in (1, 0):
        kernel_parts[layer] = kernel_terms(padded_acts[layer], grad, lat_rows, lon_cols)
        back = transpose_conv(extend(grad), conv_kernel[layer], lat_rows, lon_cols)
        grad = (grad.astype(jnp.float32) + gelu_back(states[layer].astype(jnp.float32), back)).astype(jnp.bfloat16)
    scale = 1.0 / (lat_rows * lon_cols) ** 0.5
    flat_grad = grad.reshape(-1, CH)
    obs_grad = jnp.dot(feat.T, flat_grad, preferred_element_type=jnp.float32)
    field_grad = jnp.einsum('fhw,hwc->fc', grid_fields.astype(jnp.float32), grad.astype(jnp.float32))
    return (states[2], scale * jnp.stack(kernel_parts), scale * obs_grad, scale * field_grad)
```

```python
import functools

import jax
import jax.numpy as jnp
from jax import lax
from jax.experimental import pallas as pl
from jax.experimental.pallas import tpu as pltpu
from jax.sharding import PartitionSpec as P

BF16 = jnp.bfloat16
F32 = jnp.float32
MESH = pl.DeviceIdType.MESH
TAPS = 5
SIDE = 16
ROOT = 0.7978845608028654


def gelu_pair(x):
    cubic = 0.044715 * x * x
    bend = jnp.tanh(ROOT * x * (1.0 + cubic))
    half = 0.5 * (1.0 + bend)
    slope = half + 0.5 * x * (1.0 - bend * bend) * (ROOT * (1.0 + 3.0 * cubic))
    return x * half, slope


def stage_plan(lat_parts, lon_parts, lat_first):
    lat = [("lat", 2, 1), ("lat", lat_parts // 2, 2)] if lat_parts % 2 == 0 else [("lat", lat_parts, 1)]
    lon = [("lon", 2, 1), ("lon", lon_parts // 2, 2)] if lon_parts % 2 == 0 else [("lon", lon_parts, 1)]
    if lat_first:
        plan = lat + lon
    else:
        plan = lat[:1] + lon[:1] + lat[1:] + lon[1:]
    return [stage for stage in plan if stage[1] > 1]


class Group:
    def __init__(self, stage, lat, lon):
        self.axis, self.size, self.stride = stage
        self.lat, self.lon = lat, lon
        pos = lat if self.axis == "lat" else lon
        self.rank = lax.rem(pos // self.stride, self.size)
        self.pos = pos

    def rank_at(self, dist):
        return lax.rem(self.rank + dist, self.size)

    def device(self, rank):
        pos = self.pos + (rank - self.rank) * self.stride
        return (pos, self.lon) if self.axis == "lat" else (self.lat, pos)


def kernel(
    lat_parts, lon_parts,
    fields_ref, values_ref, count_ref, cell_ref, valid_ref, dist_ref,
    field_w_ref, obs_w_ref, conv_ref, cot_ref,
    enc_ref, kgrad_ref, small_ref,
    header, vrecv, hrecv, featx, wcat, wbuf, pad_g2, pad_a1, pad_a2, pad_g1,
    left, right, turned, shifted, shifted_side, back2, x_keep, slope1, slope2,
    kacc, part, final, inbox, small, small_in,
    a2a_send, a2a_recv, own_sem, halo_send, halo_recv,
    rs_send, rs_recv, ag_send, ag_recv, sm_send, sm_recv,
):
    lat = lax.axis_index("lat")
    lon = lax.axis_index("lon")
    parts = lat_parts * lon_parts
    me = lat * lon_parts + lon
    rows, cols, channels = cot_ref.shape
    capacity = values_ref.shape[2]
    side = slice(cols, cols + SIDE)
    wide = cols + SIDE
    tile_count = part.shape[1]

    def device_at(dist):
        peer = lax.rem(me + dist, parts)
        return peer, (peer // lon_parts, lax.rem(peer, lon_parts))

    barrier = pltpu.get_barrier_semaphore()

    @pl.loop(1, parts)
    def _(dist):
        pl.semaphore_signal(barrier, inc=1, device_id=device_at(dist)[1], device_id_type=MESH)

    ii = lax.broadcasted_iota(jnp.int32, (parts, parts), 0)
    jj = lax.broadcasted_iota(jnp.int32, (parts, parts), 1)
    counts = jnp.sum(
        jnp.where(ii == jj, jnp.broadcast_to(count_ref[...], (parts, parts)), 0).astype(F32),
        axis=1, keepdims=True,
    )
    slot = lax.broadcasted_iota(jnp.int32, (parts, capacity), 1).astype(F32)
    used = (valid_ref[0] == 1) & (slot < counts)
    weight = jnp.where(used, jnp.exp(-0.5 * dist_ref[0]), 0.0).astype(BF16).astype(F32)
    header[...] = jnp.zeros_like(header)
    header[:, 0, 0:capacity] = weight
    header[:, 1, 0:capacity] = cell_ref[0].astype(F32)

    def clear_edges(pad, k):
        zero = jnp.zeros((2, wide, channels), BF16)
        zero_side = jnp.zeros((2, SIDE, channels), BF16)

        @pl.when(lat == 0)
        def _():
            pad[0:2] = zero
            left[k, 0:2] = zero_side
            right[k, 0:2] = zero_side

        @pl.when(lat == lat_parts - 1)
        def _():
            pad[rows + 2 : rows + 4] = zero
            left[k, rows + 2 : rows + 4] = zero_side
            right[k, rows + 2 : rows + 4] = zero_side

    def halo_copies(pad, k):
        up, down = lat - 1, lat + 1
        west = lax.rem(lon + lon_parts - 1, lon_parts)
        east = lax.rem(lon + 1, lon_parts)
        first, last = slice(2, 4), slice(rows, rows + 2)
        above, below = slice(0, 2), slice(rows + 2, rows + 4)
        middle = slice(2, rows + 2)
        lo, hi, full = slice(0, SIDE), slice(cols - SIDE, cols), slice(0, cols)
        has_up, has_down = lat > 0, lat < lat_parts - 1
        table = [
            (pad.at[first, full], pad.at[below, full], (up, lon), has_up, has_down),
            (pad.at[last, full], pad.at[above, full], (down, lon), has_down, has_up),
            (pad.at[middle, lo], right.at[k, middle], (lat, west), None, None),
            (pad.at[middle, hi], left.at[k, middle], (lat, east), None, None),
            (pad.at[first, lo], right.at[k, below], (up, west), has_up, has_down),
            (pad.at[first, hi], left.at[k, below], (up, east), has_up, has_down),
            (pad.at[last, lo], right.at[k, above], (down, west), has_down, has_up),
            (pad.at[last, hi], left.at[k, above], (down, east), has_down, has_up),
        ]
        out = []
        for n, (src, dst, dev, can_send, can_recv) in enumerate(table):
            copy = pltpu.make_async_remote_copy(
                src_ref=src, dst_ref=dst, send_sem=halo_send.at[k, n], recv_sem=halo_recv.at[k, n],
                device_id=dev, device_id_type=MESH,
            )
            out.append((copy, can_send, can_recv))
        return out

    def guarded(cond, act):
        if cond is None:
            act()
        else:
            pl.when(cond)(act)

    def halo_start(copies):
        for copy, can_send, _ in copies:
            guarded(can_send, copy.start)

    def halo_finish(copies, pad, k):
        for copy, _, can_recv in copies:
            guarded(can_recv, copy.wait_recv)
        at = lax.broadcasted_iota(jnp.int32, (SIDE, channels), 0)

        @pl.loop(0, rows + 4)
        def _(h):
            r = right[k, h].astype(F32)
            l = left[k, h].astype(F32)
            pad[h, side] = jnp.where(at < 2, r, jnp.where(at >= SIDE - 2, l, 0.0)).astype(BF16)

    def halo_drain(copies):
        for copy, can_send, _ in copies:
            guarded(can_send, copy.wait_send)

    def place_weights(layer, turn):
        for p in range(TAPS):
            for q in range(TAPS):
                if turn:
                    block = conv_ref[layer, TAPS - 1 - p, TAPS - 1 - q].T
                else:
                    block = conv_ref[layer, p, q]
                wbuf[p * channels : (p + 1) * channels, q * channels : (q + 1) * channels] = block

    group = 4 if rows % 4 == 0 else 1

    def conv(pad, finish):
        @pl.loop(0, rows // group)
        def _(b):
            lhs = jnp.concatenate(
                [pad[pl.ds(b * group + p, group)].reshape(group * wide, channels) for p in range(TAPS)],
                axis=1,
            )
            prod = jnp.dot(lhs, wbuf[...], preferred_element_type=F32)
            for r in range(group):
                total = None
                for q in range(TAPS):
                    piece = prod[r * wide : (r + 1) * wide, q * channels : (q + 1) * channels]
                    shift = (2 - q) % wide
                    if shift:
                        piece = pltpu.roll(piece, shift, 0)
                    piece = piece[:cols]
                    total = piece if total is None else total + piece
                finish(b * group + r, total)

    def shift_grad(pad):
        @pl.loop(0, rows)
        def _(h):
            ext = jnp.concatenate(
                [pad[h + 2, 0:cols].astype(F32), jnp.zeros((SIDE, channels), F32)], axis=0
            )
            for q in range(TAPS):
                shift = (q - 2) % wide
                moved = (pltpu.roll(ext, shift, 0) if shift else ext).astype(BF16)
                lanes = slice(q * channels, (q + 1) * channels)
                shifted[h, :, lanes] = moved[:cols]
                shifted_side[h, :, lanes] = moved[cols:]

    def turn_act(pad):
        @pl.loop(0, rows + 4)
        def _(h):
            turned[h] = pad[h, 0:cols].T

    def kernel_terms(pad, slot_of):
        side_lhs = jnp.concatenate(
            [pad[p : p + rows, side].reshape(rows * SIDE, channels).T for p in range(TAPS)], axis=0
        )
        kacc[...] = jnp.dot(
            side_lhs, shifted_side[...].reshape(rows * SIDE, TAPS * channels),
            preferred_element_type=F32,
        )

        @pl.loop(0, rows // group)
        def _(b):
            lhs = jnp.concatenate(
                [
                    jnp.concatenate([turned[b * group + p + r] for r in range(group)], axis=1)
                    for p in range(TAPS)
                ],
                axis=0,
            )
            rhs = shifted[pl.ds(b * group, group)].reshape(group * cols, TAPS * channels)
            kacc[...] += jnp.dot(lhs, rhs, preferred_element_type=F32)

        per = channels // 16
        for p in range(TAPS):
            for q in range(TAPS):
                block = kacc[p * channels : (p + 1) * channels, q * channels : (q + 1) * channels]
                n = (p * TAPS + q) * per
                part[slot_of, n : n + per] = block.astype(BF16).reshape(per, 16, channels)
        used_tiles = TAPS * TAPS * per
        if used_tiles < tile_count:
            part[slot_of, used_tiles:] = jnp.zeros(
                (tile_count - used_tiles, 16, channels), BF16
            )

    def sum_steps(slot_of, plan):
        groups = [Group(stage, lat, lon) for stage in plan]
        pending = []
        base = jnp.int32(0)
        length = tile_count
        box = 0
        nsem = 0
        bases = []
        for g in groups:
            share = length // g.size
            sent = []
            for dist in range(1, g.size):
                copy = pltpu.make_async_remote_copy(
                    src_ref=part.at[slot_of, pl.ds(base + g.rank_at(dist) * share, share)],
                    dst_ref=inbox.at[slot_of, pl.ds(box + (dist - 1) * share, share)],
                    send_sem=rs_send.at[slot_of, nsem], recv_sem=rs_recv.at[slot_of, nsem],
                    device_id=g.device(g.rank_at(dist)), device_id_type=MESH,
                )
                copy.start()
                sent.append(copy)
                nsem += 1
            pending += sent
            yield
            for copy in sent:
                copy.wait_recv()
            mine = base + g.rank * share
            total = part[slot_of, pl.ds(mine, share)].astype(F32)
            for dist in range(1, g.size):
                at = box + (dist - 1) * share
                total = total + inbox[slot_of, at : at + share].astype(F32)
            part[slot_of, pl.ds(mine, share)] = total.astype(BF16)
            box += (g.size - 1) * share
            bases.append(base)
            base, length = mine, share
        final[slot_of, pl.ds(base, length)] = part[slot_of, pl.ds(base, length)]
        nsem = 0
        for g, low in zip(reversed(groups), reversed(bases)):
            sent, got = [], []
            for dist in range(1, g.size):
                copy = pltpu.make_async_remote_copy(
                    src_ref=final.at[slot_of, pl.ds(base, length)],
                    dst_ref=final.at[slot_of, pl.ds(base, length)],
                    send_sem=ag_send.at[slot_of, nsem], recv_sem=ag_recv.at[slot_of, nsem],
                    device_id=g.device(g.rank_at(dist)), device_id_type=MESH,
                )
                copy.start()
                sent.append(copy)
                here = final.at[slot_of, pl.ds(low + g.rank_at(g.size - dist) * length, length)]
                got.append(
                    pltpu.make_async_remote_copy(
                        src_ref=here, dst_ref=here,
                        send_sem=ag_send.at[slot_of, nsem], recv_sem=ag_recv.at[slot_of, nsem],
                        device_id=g.device(g.rank_at(dist)), device_id_type=MESH,
                    )
                )
                nsem += 1
            pending += sent
            yield
            for copy in got:
                copy.wait_recv()
            base, length = low, length * g.size
        for copy in pending:
            copy.wait_send()
        kgrad_ref[slot_of] = final[slot_of]

    def small_steps(plan):
        nsem = 0
        pending = []
        for n, stage in enumerate(plan):
            g = Group(stage, lat, lon)
            sent = []
            for dist in range(1, g.size):
                copy = pltpu.make_async_remote_copy(
                    src_ref=small.at[n], dst_ref=small_in.at[nsem],
                    send_sem=sm_send.at[nsem], recv_sem=sm_recv.at[nsem],
                    device_id=g.device(g.rank_at(dist)), device_id_type=MESH,
                )
                copy.start()
                sent.append((copy, nsem, dist))
                nsem += 1
            pending += sent
            yield
            for copy, _, _ in sent:
                copy.wait_recv()
            total = jnp.zeros(small.shape[1:], F32)
            mine = small[n].astype(F32)
            for rank in range(g.size):
                term = mine
                for _, box, dist in sent:
                    term = jnp.where(g.rank_at(g.size - dist) == rank, small_in[box].astype(F32), term)
                total = total + term
            small[n + 1] = total.astype(BF16)
        for copy, _, _ in pending:
            copy.wait_send()
        small_ref[...] = small[len(plan)]

    pad_g2[2 : rows + 2, 0:cols] = cot_ref[...]
    for k, pad in enumerate((pad_g2, pad_a1, pad_a2, pad_g1)):
        clear_edges(pad, k)
    place_weights(1, True)
    field_count = fields_ref.shape[0]
    width = values_ref.shape[3]
    featx[width:, :] = jnp.zeros((featx.shape[0] - width, featx.shape[1]), BF16)
    featx[width : width + field_count, :] = fields_ref[...]
    wcat[...] = jnp.zeros_like(wcat)
    wcat[0:width] = obs_w_ref[...]
    wcat[width : width + field_count] = field_w_ref[...]

    pl.semaphore_wait(barrier, parts - 1)

    own = pltpu.make_async_copy(values_ref.at[0, me], vrecv.at[me], own_sem.at[0])
    own.start()
    own_head = pltpu.make_async_copy(header.at[me], hrecv.at[me], own_sem.at[1])
    own_head.start()

    def row_copies(dist):
        peer, dev = device_at(dist)
        return [
            pltpu.make_async_remote_copy(
                src_ref=src, dst_ref=dst, send_sem=a2a_send.at[n, dist], recv_sem=a2a_recv.at[n, dist],
                device_id=dev, device_id_type=MESH,
            )
            for n, (src, dst) in enumerate(
                ((values_ref.at[0, peer], vrecv.at[me]), (header.at[peer], hrecv.at[me]))
            )
        ]

    @pl.loop(1, parts)
    def _(dist):
        for copy in row_copies(dist):
            copy.start()

    halo_g2 = halo_copies(pad_g2, 0)
    halo_start(halo_g2)
    halo_finish(halo_g2, pad_g2, 0)

    def keep_back(h, total):
        back2[h] = total

    conv(pad_g2, keep_back)
    place_weights(0, False)

    own.wait()
    own_head.wait()

    @pl.loop(1, parts)
    def _(dist):
        sender = lax.rem(me + parts - dist, parts)
        for n, dst in enumerate((vrecv.at[sender], hrecv.at[sender])):
            pltpu.make_async_remote_copy(
                src_ref=dst, dst_ref=dst, send_sem=a2a_send.at[n, dist], recv_sem=a2a_recv.at[n, dist],
                device_id=device_at(dist)[1], device_id_type=MESH,
            ).wait_recv()

    count = parts * capacity
    lane = lax.broadcasted_iota(jnp.int32, (count, 128), 1)
    pick = lane == lax.rem(lax.broadcasted_iota(jnp.int32, (count, 128), 0), capacity)

    def column(n):
        spread = jnp.broadcast_to(hrecv[:, n : n + 1, :], (parts, capacity, 128)).reshape(count, 128)
        return jnp.sum(jnp.where(pick, spread, 0.0), axis=1, keepdims=True)

    w_col, cell_col = column(0), column(1)
    values_t = jnp.concatenate(
        [vrecv[...].reshape(count, width).T, jnp.ones((16, count), BF16)], axis=0
    )
    block = 512 if (rows * cols) % 512 == 0 else cols

    @pl.loop(0, rows * cols // block)
    def _(b):
        start = pl.multiple_of(b * block, block)
        ids = (start + lax.broadcasted_iota(jnp.int32, (count, block), 1)).astype(F32)
        spread = jnp.where(ids == cell_col, w_col, 0.0).astype(BF16)
        sums = jnp.dot(values_t, spread, preferred_element_type=F32)
        dens = sums[width : width + 1]
        featx[0:width, pl.ds(start, block)] = (sums[0:width] / (1.0 + dens)).astype(BF16)

    @pl.loop(0, rows)
    def _(h):
        start = pl.multiple_of(h * cols, cols)
        feats = featx[:, pl.ds(start, cols)].T
        x = jnp.dot(feats, wcat[...], preferred_element_type=F32).astype(BF16).astype(F32)
        act, slope = gelu_pair(x)
        x_keep[h] = x
        slope1[h] = slope
        pad_a1[h + 2, 0:cols] = act.astype(BF16)

    halo_a1 = halo_copies(pad_a1, 1)
    halo_start(halo_a1)
    halo_finish(halo_a1, pad_a1, 1)

    def first_layer(h, total):
        x = (x_keep[h] + total).astype(BF16).astype(F32)
        act, slope = gelu_pair(x)
        x_keep[h] = x
        pad_a2[h + 2, 0:cols] = act.astype(BF16)
        g = cot_ref[h].astype(F32) + slope * back2[h]
        pad_g1[h + 2, 0:cols] = g.astype(BF16)

    conv(pad_a1, first_layer)
    halo_a2 = halo_copies(pad_a2, 2)
    halo_start(halo_a2)
    halo_g1 = halo_copies(pad_g1, 3)
    halo_start(halo_g1)

    turn_act(pad_a1)
    shift_grad(pad_g1)
    kernel_terms(pad_a1, 0)
    sum_a = sum_steps(0, stage_plan(lat_parts, lon_parts, True))
    next(sum_a)

    halo_finish(halo_a2, pad_a2, 2)
    turn_act(pad_a2)
    shift_grad(pad_g2)
    next(sum_a, None)
    kernel_terms(pad_a2, 1)
    sum_b = sum_steps(1, stage_plan(lat_parts, lon_parts, False))
    next(sum_b)
    next(sum_a, None)

    place_weights(0, True)
    halo_finish(halo_g1, pad_g1, 3)

    def last_grad(h, total):
        g = pad_g1[h + 2, 0:cols].astype(F32) + slope1[h] * total
        back2[h] = g

    conv(pad_g1, last_grad)
    next(sum_b, None)
    grads = jnp.dot(
        featx[...], back2[...].astype(BF16).reshape(rows * cols, channels), preferred_element_type=F32
    )
    small[0] = grads[0 : small.shape[1]].astype(BF16)
    sum_c = small_steps(stage_plan(lat_parts, lon_parts, True))
    next(sum_c)
    next(sum_a, None)
    next(sum_b, None)

    place_weights(1, False)

    def last_layer(h, total):
        enc_ref[h] = (x_keep[h] + total).astype(BF16)

    conv(pad_a2, last_layer)

    live = [sum_c, sum_a, sum_b]
    while live:
        live = [s for s in live if next(s, "end") != "end"]

    for copies in (halo_g2, halo_a1, halo_a2, halo_g1):
        halo_drain(copies)

    @pl.loop(1, parts)
    def _(dist):
        for copy in row_copies(dist):
            copy.wait_send()


def per_device(
    grid_fields, obs_values, obs_count, obs_cell, obs_valid, obs_dist2,
    field_weight, obs_weight, conv_kernel, cotangent,
):
    rows, cols, channels = cotangent.shape
    lat_parts = lax.axis_size("lat")
    lon_parts = lax.axis_size("lon")
    parts = lat_parts * lon_parts
    fields = grid_fields.shape[0]
    width = obs_values.shape[3]
    capacity = obs_values.shape[2]
    wide = cols + SIDE
    tiles = TAPS * TAPS * channels // 16
    tiles = -(-tiles // parts) * parts
    plan = stage_plan(lat_parts, lon_parts, True)
    hops = sum(stage[1] - 1 for stage in plan)
    deep = -(-(width + fields) // 128) * 128
    small_rows = -(-(width + fields) // 16) * 16
    vmem = pl.BlockSpec(memory_space=pltpu.VMEM)
    pads = [pltpu.VMEM((rows + 4, wide, channels), BF16)] * 4
    encoded, kgrad, small = pl.pallas_call(
        functools.partial(kernel, lat_parts, lon_parts),
        out_shape=(
            jax.ShapeDtypeStruct((rows, cols, channels), BF16),
            jax.ShapeDtypeStruct((2, tiles, 16, channels), BF16),
            jax.ShapeDtypeStruct((small_rows, channels), BF16),
        ),
        in_specs=[vmem] * 10,
        out_specs=(vmem, vmem, vmem),
        scratch_shapes=[
            pltpu.VMEM((parts, 2, 128), F32),
            pltpu.VMEM((parts, capacity, width), BF16),
            pltpu.VMEM((parts, 2, 128), F32),
            pltpu.VMEM((deep, rows * cols), BF16),
            pltpu.VMEM((deep, channels), BF16),
            pltpu.VMEM((TAPS * channels, TAPS * channels), BF16),
            *pads,
            pltpu.VMEM((4, rows + 4, SIDE, channels), BF16),
            pltpu.VMEM((4, rows + 4, SIDE, channels), BF16),
            pltpu.VMEM((rows + 4, channels, cols), BF16),
            pltpu.VMEM((rows, cols, TAPS * channels), BF16),
            pltpu.VMEM((rows, SIDE, TAPS * channels), BF16),
            pltpu.VMEM((rows, cols, channels), F32),
            pltpu.VMEM((rows, cols, channels), F32),
            pltpu.VMEM((rows, cols, channels), F32),
            pltpu.VMEM((rows, cols, channels), F32),
            pltpu.VMEM((TAPS * channels, TAPS * channels), F32),
            pltpu.VMEM((2, tiles, 16, channels), BF16),
            pltpu.VMEM((2, tiles, 16, channels), BF16),
            pltpu.VMEM((2, tiles, 16, channels), BF16),
            pltpu.VMEM((len(plan) + 1, small_rows, channels), BF16),
            pltpu.VMEM((hops, small_rows, channels), BF16),
            pltpu.SemaphoreType.DMA((2, parts)),
            pltpu.SemaphoreType.DMA((2, parts)),
            pltpu.SemaphoreType.DMA((2,)),
            pltpu.SemaphoreType.DMA((4, 8)),
            pltpu.SemaphoreType.DMA((4, 8)),
            pltpu.SemaphoreType.DMA((2, hops)),
            pltpu.SemaphoreType.DMA((2, hops)),
            pltpu.SemaphoreType.DMA((2, hops)),
            pltpu.SemaphoreType.DMA((2, hops)),
            pltpu.SemaphoreType.DMA((hops,)),
            pltpu.SemaphoreType.DMA((hops,)),
        ],
        compiler_params=pltpu.CompilerParams(
            collective_id=0, has_side_effects=True, vmem_limit_bytes=56 * 1024 * 1024
        ),
        name="encoder",
    )(
        grid_fields.reshape(fields, rows * cols), obs_values, obs_count, obs_cell, obs_valid,
        obs_dist2, field_weight, obs_weight, conv_kernel, cotangent,
    )
    scale = 1.0 / (rows * lat_parts * cols * lon_parts) ** 0.5
    used = TAPS * TAPS * channels // 16
    kernel_grad = scale * kgrad[:, :used].astype(F32).reshape(2, TAPS, TAPS, channels, channels)
    small = scale * small.astype(F32)
    return encoded, kernel_grad, small[:width], small[width : width + fields]


def solution(mesh):
    return jax.shard_map(
        per_device,
        mesh=mesh,
        in_specs=(
            P(None, "lat", "lon"),
            P(("lat", "lon"), None, None, None),
            P(("lat", "lon"), None),
            P(("lat", "lon"), None, None),
            P(("lat", "lon"), None, None),
            P(("lat", "lon"), None, None),
            P(),
            P(),
            P(),
            P("lat", "lon", None),
        ),
        out_specs=(P("lat", "lon", None), P(), P(), P()),
        check_vma=False,
    )
```

```python
import functools
import math

import jax
import jax.numpy as jnp
from jax import lax
from jax.experimental import pallas as pl
from jax.experimental.pallas import tpu as pltpu
from jax.sharding import PartitionSpec as P

BF16 = jnp.bfloat16
F32 = jnp.float32
MESH = pl.DeviceIdType.MESH
TAPS = 5
SIDE = 16
ROOT = 0.7978845608028654


def gelu_pair(x):
    cubic = 0.044715 * x * x
    bend = jnp.tanh(ROOT * x * (1.0 + cubic))
    half = 0.5 * (1.0 + bend)
    slope = half + 0.5 * x * (1.0 - bend * bend) * (ROOT * (1.0 + 3.0 * cubic))
    return x * half, slope


def stage_plan(lat_parts, lon_parts, lat_first):
    lat = [("lat", 2, 1), ("lat", lat_parts // 2, 2)] if lat_parts % 2 == 0 else [("lat", lat_parts, 1)]
    lon = [("lon", 2, 1), ("lon", lon_parts // 2, 2)] if lon_parts % 2 == 0 else [("lon", lon_parts, 1)]
    if lat_first:
        plan = lat + lon
    else:
        plan = lat[:1] + lon[:1] + lat[1:] + lon[1:]
    return [stage for stage in plan if stage[1] > 1]


class Group:
    def __init__(self, stage, lat, lon):
        self.axis, self.size, self.stride = stage
        self.lat, self.lon = lat, lon
        pos = lat if self.axis == "lat" else lon
        self.rank = lax.rem(pos // self.stride, self.size)
        self.pos = pos

    def rank_at(self, dist):
        return lax.rem(self.rank + dist, self.size)

    def device(self, rank):
        pos = self.pos + (rank - self.rank) * self.stride
        return (pos, self.lon) if self.axis == "lat" else (self.lat, pos)


def kernel(
    lat_parts, lon_parts,
    fields_ref, values_ref, count_ref, cell_ref, valid_ref, dist_ref,
    field_w_ref, obs_w_ref, conv_ref, cot_ref,
    enc_ref, kgrad_ref, small_ref,
    header, vrecv, hrecv, featx, wcat, wbuf, pad_g2, pad_a1, pad_a2, pad_g1,
    left, right, strip_out, strip_in, strip_w, strip_e, strip_z, field_rows,
    turned, shifted, shifted_side, back2, x_keep, slope1,
    kacc, part, final, inbox, small, small_in,
    a2a_send, a2a_recv, own_sem, halo_send, halo_recv,
    rs_send, rs_recv, ag_send, ag_recv, sm_send, sm_recv,
):
    lat = lax.axis_index("lat")
    lon = lax.axis_index("lon")
    parts = lat_parts * lon_parts
    me = lat * lon_parts + lon
    rows, cols, channels = cot_ref.shape
    capacity = values_ref.shape[2]
    side = slice(cols, cols + SIDE)
    wide = cols + SIDE
    tile_count = part.shape[1]

    def device_at(dist):
        peer = lax.rem(me + dist, parts)
        return peer, (peer // lon_parts, lax.rem(peer, lon_parts))

    barrier = pltpu.get_barrier_semaphore()

    @pl.loop(1, parts)
    def _(dist):
        pl.semaphore_signal(barrier, inc=1, device_id=device_at(dist)[1], device_id_type=MESH)

    slot = lax.broadcasted_iota(jnp.int32, (capacity, parts), 0)
    used = (valid_ref[0] == 1) & (slot < count_ref[...])
    weight = jnp.where(used, jnp.exp(-0.5 * dist_ref[0]), 0.0).astype(BF16).astype(F32)
    header[...] = jnp.zeros_like(header)
    header[:, 0, 0:capacity] = weight.T
    header[:, 1, 0:capacity] = cell_ref[0].astype(F32).T

    def clear_edges(pad, k):
        zero = jnp.zeros((2, wide, channels), BF16)
        zero_side = jnp.zeros((2, SIDE, channels), BF16)

        @pl.when(lat == 0)
        def _():
            pad[0:2] = zero
            left[k, 0:2] = zero_side
            right[k, 0:2] = zero_side

        @pl.when(lat == lat_parts - 1)
        def _():
            pad[rows + 2 : rows + 4] = zero
            left[k, 2:4] = zero_side
            right[k, 2:4] = zero_side

    def halo_copies(pad, k):
        up, down = lat - 1, lat + 1
        west = lax.rem(lon + lon_parts - 1, lon_parts)
        east = lax.rem(lon + 1, lon_parts)
        first, last = slice(2, 4), slice(rows, rows + 2)
        above, below = slice(0, 2), slice(rows + 2, rows + 4)
        top, bottom = slice(0, 2), slice(2, 4)
        lo, hi, full = slice(0, SIDE), slice(cols - SIDE, cols), slice(0, cols)
        has_up, has_down = lat > 0, lat < lat_parts - 1
        table = [
            (pad.at[first, full], pad.at[below, full], (up, lon), has_up, has_down),
            (pad.at[last, full], pad.at[above, full], (down, lon), has_down, has_up),
            (strip_out.at[k, 0], strip_in.at[k, 0], (lat, west), None, None),
            (strip_out.at[k, 1], strip_in.at[k, 1], (lat, east), None, None),
            (pad.at[first, lo], right.at[k, bottom], (up, west), has_up, has_down),
            (pad.at[first, hi], left.at[k, bottom], (up, east), has_up, has_down),
            (pad.at[last, lo], right.at[k, top], (down, west), has_down, has_up),
            (pad.at[last, hi], left.at[k, top], (down, east), has_down, has_up),
        ]
        out = []
        for n, (src, dst, dev, can_send, can_recv) in enumerate(table):
            copy = pltpu.make_async_remote_copy(
                src_ref=src, dst_ref=dst, send_sem=halo_send.at[k, n], recv_sem=halo_recv.at[k, n],
                device_id=dev, device_id_type=MESH,
            )
            out.append((copy, can_send, can_recv))
        return out

    def guarded(cond, act):
        if cond is None:
            act()
        else:
            pl.when(cond)(act)

    def halo_start(copies, pad, k):
        for copy, can_send, _ in copies[:2]:
            guarded(can_send, copy.start)
        for copy, can_send, _ in copies[4:]:
            guarded(can_send, copy.start)
        strip_w[...] = pad[2 : rows + 2, 0:SIDE].reshape(rows * SIDE, channels).astype(F32)
        strip_e[...] = (
            pad[2 : rows + 2, cols - SIDE : cols].reshape(rows * SIDE, channels).astype(F32)
        )
        for j in range(2):
            strip_out[k, 0, j] = strip_w[pl.ds(j, rows, stride=SIDE)].astype(BF16)
            strip_out[k, 1, j] = strip_e[pl.ds(SIDE - 2 + j, rows, stride=SIDE)].astype(BF16)
        for copy, can_send, _ in copies[2:4]:
            guarded(can_send, copy.start)

    def halo_finish(copies, pad, k):
        for copy, _, can_recv in copies:
            guarded(can_recv, copy.wait_recv)
        for j in range(2):
            strip_z[pl.ds(j, rows, stride=SIDE)] = strip_in[k, 0, j].astype(F32)
            strip_z[pl.ds(SIDE - 2 + j, rows, stride=SIDE)] = strip_in[k, 1, j].astype(F32)
        pad[2 : rows + 2, side] = strip_z[...].astype(BF16).reshape(rows, SIDE, channels)
        at = lax.broadcasted_iota(jnp.int32, (4, SIDE, channels), 1)
        corner = jnp.where(
            at < 2, right[k].astype(F32), jnp.where(at >= SIDE - 2, left[k].astype(F32), 0.0)
        ).astype(BF16)
        pad[0:2, side] = corner[0:2]
        pad[rows + 2 : rows + 4, side] = corner[2:4]

    def halo_drain(copies):
        for copy, can_send, _ in copies:
            guarded(can_send, copy.wait_send)

    def place_weights(layer, turn):
        at = 2 * layer + turn
        for p in range(TAPS):
            for q in range(TAPS):
                if turn:
                    block = conv_ref[layer, TAPS - 1 - p, TAPS - 1 - q].T
                else:
                    block = conv_ref[layer, p, q]
                wbuf[at, p * channels : (p + 1) * channels, q * channels : (q + 1) * channels] = block

    group = 4 if rows % 4 == 0 else 1

    def conv(pad, at, finish, between=None):
        def one(b):
            lhs = jnp.concatenate(
                [pad[pl.ds(b * group + p, group)].reshape(group * wide, channels) for p in range(TAPS)],
                axis=1,
            )
            prod = jnp.dot(lhs, wbuf[at], preferred_element_type=F32)
            for r in range(group):
                total = None
                for q in range(TAPS):
                    piece = prod[r * wide : (r + 1) * wide, q * channels : (q + 1) * channels]
                    shift = (2 - q) % wide
                    if shift:
                        piece = pltpu.roll(piece, shift, 0)
                    piece = piece[:cols]
                    total = piece if total is None else total + piece
                finish(b * group + r, total)

        if between is None:
            pl.loop(0, rows // group)(one)
        else:
            for b in range(rows // group):
                one(b)
                between()

    def shift_grad(pad, at):
        @pl.loop(0, rows)
        def _(h):
            ext = jnp.concatenate(
                [pad[h + 2, 0:cols].astype(F32), jnp.zeros((SIDE, channels), F32)], axis=0
            )
            for q in range(TAPS):
                shift = (q - 2) % wide
                moved = (pltpu.roll(ext, shift, 0) if shift else ext).astype(BF16)
                lanes = slice(q * channels, (q + 1) * channels)
                shifted[at, h, :, lanes] = moved[:cols]
                shifted_side[at, h, :, lanes] = moved[cols:]

    def turn_act(pad):
        @pl.loop(2, rows + 2)
        def _(h):
            turned[h] = pad[h, 0:cols].T

    def turn_halo(pad):
        for h in (0, 1, rows + 2, rows + 3):
            turned[h] = pad[h, 0:cols].T

    def kernel_terms(pad, slot_of, between=None):
        side_lhs = jnp.concatenate(
            [pad[p : p + rows, side].reshape(rows * SIDE, channels).T for p in range(TAPS)], axis=0
        )
        kacc[...] = jnp.dot(
            side_lhs, shifted_side[slot_of].reshape(rows * SIDE, TAPS * channels),
            preferred_element_type=F32,
        )

        def one(b):
            lhs = jnp.concatenate(
                [
                    jnp.concatenate([turned[b * group + p + r] for r in range(group)], axis=1)
                    for p in range(TAPS)
                ],
                axis=0,
            )
            rhs = shifted[slot_of, pl.ds(b * group, group)].reshape(group * cols, TAPS * channels)
            kacc[...] += jnp.dot(lhs, rhs, preferred_element_type=F32)

        if between is None:
            pl.loop(0, rows // group)(one)
        else:
            for b in range(rows // group):
                one(b)
                between()
        per = channels // 16
        for p in range(TAPS):
            for q in range(TAPS):
                block = kacc[p * channels : (p + 1) * channels, q * channels : (q + 1) * channels]
                n = (p * TAPS + q) * per
                part[slot_of, n : n + per] = block.astype(BF16).reshape(per, 16, channels)
        used_tiles = TAPS * TAPS * per
        if used_tiles < tile_count:
            part[slot_of, used_tiles:] = jnp.zeros(
                (tile_count - used_tiles, 16, channels), BF16
            )

    def sum_steps(slot_of, start, length, stream, plan):
        groups = [Group(stage, lat, lon) for stage in plan]
        pending = []
        base = start
        box = start
        whole = slice(start, start + length)
        nsem = 0
        bases = []
        for g in groups:
            share = length // g.size
            sent = []
            for dist in range(1, g.size):
                copy = pltpu.make_async_remote_copy(
                    src_ref=part.at[slot_of, pl.ds(base + g.rank_at(dist) * share, share)],
                    dst_ref=inbox.at[slot_of, pl.ds(box + (dist - 1) * share, share)],
                    send_sem=rs_send.at[stream, nsem], recv_sem=rs_recv.at[stream, nsem],
                    device_id=g.device(g.rank_at(dist)), device_id_type=MESH,
                )
                copy.start()
                sent.append(copy)
                nsem += 1
            pending += sent
            yield
            for copy in sent:
                copy.wait_recv()
            mine = base + g.rank * share
            total = part[slot_of, pl.ds(mine, share)].astype(F32)
            for dist in range(1, g.size):
                at = box + (dist - 1) * share
                total = total + inbox[slot_of, at : at + share].astype(F32)
            part[slot_of, pl.ds(mine, share)] = total.astype(BF16)
            box += (g.size - 1) * share
            bases.append(base)
            base, length = mine, share
        final[slot_of, pl.ds(base, length)] = part[slot_of, pl.ds(base, length)]
        nsem = 0
        for g, low in zip(reversed(groups), reversed(bases)):
            sent, got = [], []
            for dist in range(1, g.size):
                copy = pltpu.make_async_remote_copy(
                    src_ref=final.at[slot_of, pl.ds(base, length)],
                    dst_ref=final.at[slot_of, pl.ds(base, length)],
                    send_sem=ag_send.at[stream, nsem], recv_sem=ag_recv.at[stream, nsem],
                    device_id=g.device(g.rank_at(dist)), device_id_type=MESH,
                )
                copy.start()
                sent.append(copy)
                here = final.at[slot_of, pl.ds(low + g.rank_at(g.size - dist) * length, length)]
                got.append(
                    pltpu.make_async_remote_copy(
                        src_ref=here, dst_ref=here,
                        send_sem=ag_send.at[stream, nsem], recv_sem=ag_recv.at[stream, nsem],
                        device_id=g.device(g.rank_at(dist)), device_id_type=MESH,
                    )
                )
                nsem += 1
            pending += sent
            yield
            for copy in got:
                copy.wait_recv()
            base, length = low, length * g.size
        for copy in pending:
            copy.wait_send()
        kgrad_ref[slot_of, whole] = final[slot_of, whole]

    def small_steps(plan):
        nsem = 0
        pending = []
        for n, stage in enumerate(plan):
            g = Group(stage, lat, lon)
            sent = []
            for dist in range(1, g.size):
                copy = pltpu.make_async_remote_copy(
                    src_ref=small.at[n], dst_ref=small_in.at[nsem],
                    send_sem=sm_send.at[nsem], recv_sem=sm_recv.at[nsem],
                    device_id=g.device(g.rank_at(dist)), device_id_type=MESH,
                )
                copy.start()
                sent.append((copy, nsem, dist))
                nsem += 1
            pending += sent
            yield
            for copy, _, _ in sent:
                copy.wait_recv()
            total = jnp.zeros(small.shape[1:], F32)
            mine = small[n].astype(F32)
            for rank in range(g.size):
                term = mine
                for _, box, dist in sent:
                    term = jnp.where(g.rank_at(g.size - dist) == rank, small_in[box].astype(F32), term)
                total = total + term
            small[n + 1] = total.astype(BF16)
        for copy, _, _ in pending:
            copy.wait_send()
        small_ref[...] = small[len(plan)]

    pad_g2[2 : rows + 2, 0:cols] = cot_ref[...]
    for k, pad in enumerate((pad_g2, pad_a1, pad_a2, pad_g1)):
        clear_edges(pad, k)
    strip_z[...] = jnp.zeros_like(strip_z)
    place_weights(1, True)
    field_count = fields_ref.shape[0]
    width = values_ref.shape[3]
    featx[width:, :] = jnp.zeros((featx.shape[0] - width, featx.shape[1]), BF16)
    field_rows[...] = fields_ref[...].astype(F32).reshape(field_count * rows, cols)
    for h in range(rows):
        featx[width : width + field_count, h * cols : (h + 1) * cols] = field_rows[
            pl.ds(h, field_count, stride=rows)
        ].astype(BF16)
    wcat[...] = jnp.zeros_like(wcat)
    wcat[0:width] = obs_w_ref[...]
    wcat[width : width + field_count] = field_w_ref[...]

    pl.semaphore_wait(barrier, parts - 1)

    own = pltpu.make_async_copy(values_ref.at[0, me], vrecv.at[me], own_sem.at[0])
    own.start()
    own_head = pltpu.make_async_copy(header.at[me], hrecv.at[me], own_sem.at[1])
    own_head.start()

    def row_copies(dist):
        peer, dev = device_at(dist)
        return [
            pltpu.make_async_remote_copy(
                src_ref=src, dst_ref=dst, send_sem=a2a_send.at[n, dist], recv_sem=a2a_recv.at[n, dist],
                device_id=dev, device_id_type=MESH,
            )
            for n, (src, dst) in enumerate(
                ((values_ref.at[0, peer], vrecv.at[me]), (header.at[peer], hrecv.at[me]))
            )
        ]

    @pl.loop(1, parts)
    def _(dist):
        for copy in row_copies(dist):
            copy.start()

    halo_g2 = halo_copies(pad_g2, 0)
    halo_start(halo_g2, pad_g2, 0)
    shift_grad(pad_g2, 1)
    place_weights(0, False)
    halo_finish(halo_g2, pad_g2, 0)

    def keep_back(h, total):
        back2[h] = total

    conv(pad_g2, 3, keep_back)

    own.wait()
    own_head.wait()

    @pl.loop(1, parts)
    def _(dist):
        sender = lax.rem(me + parts - dist, parts)
        for n, dst in enumerate((vrecv.at[sender], hrecv.at[sender])):
            pltpu.make_async_remote_copy(
                src_ref=dst, dst_ref=dst, send_sem=a2a_send.at[n, dist], recv_sem=a2a_recv.at[n, dist],
                device_id=device_at(dist)[1], device_id_type=MESH,
            ).wait_recv()

    count = parts * capacity
    lane = lax.broadcasted_iota(jnp.int32, (count, 128), 1)
    pick = lane == lax.rem(lax.broadcasted_iota(jnp.int32, (count, 128), 0), capacity)

    def column(n):
        spread = jnp.broadcast_to(hrecv[:, n : n + 1, :], (parts, capacity, 128)).reshape(count, 128)
        return jnp.sum(jnp.where(pick, spread, 0.0), axis=1, keepdims=True)

    w_col, cell_col = column(0), column(1)
    values_t = jnp.concatenate(
        [vrecv[...].reshape(count, width).T, jnp.ones((16, count), BF16)], axis=0
    )
    block = 512 if (rows * cols) % 512 == 0 else cols

    @pl.loop(0, rows * cols // block)
    def _(b):
        start = pl.multiple_of(b * block, block)
        ids = (start + lax.broadcasted_iota(jnp.int32, (count, block), 1)).astype(F32)
        spread = jnp.where(ids == cell_col, w_col, 0.0).astype(BF16)
        sums = jnp.dot(values_t, spread, preferred_element_type=F32)
        dens = sums[width : width + 1]
        featx[0:width, pl.ds(start, block)] = (sums[0:width] / (1.0 + dens)).astype(BF16)

    @pl.loop(0, rows)
    def _(h):
        start = pl.multiple_of(h * cols, cols)
        feats = featx[:, pl.ds(start, cols)].T
        x = jnp.dot(feats, wcat[...], preferred_element_type=F32).astype(BF16).astype(F32)
        act, slope = gelu_pair(x)
        x_keep[h] = x
        slope1[h] = slope
        pad_a1[h + 2, 0:cols] = act.astype(BF16)

    halo_a1 = halo_copies(pad_a1, 1)
    halo_start(halo_a1, pad_a1, 1)
    turn_act(pad_a1)
    place_weights(0, True)
    place_weights(1, False)
    halo_finish(halo_a1, pad_a1, 1)
    turn_halo(pad_a1)

    def first_layer(h, total):
        x = (x_keep[h] + total).astype(BF16).astype(F32)
        act, slope = gelu_pair(x)
        x_keep[h] = x
        pad_a2[h + 2, 0:cols] = act.astype(BF16)
        g = cot_ref[h].astype(F32) + slope * back2[h]
        pad_g1[h + 2, 0:cols] = g.astype(BF16)

    conv(pad_a1, 0, first_layer)
    halo_a2 = halo_copies(pad_a2, 2)
    halo_start(halo_a2, pad_a2, 2)
    halo_g1 = halo_copies(pad_g1, 3)
    halo_start(halo_g1, pad_g1, 3)

    lat_plan = stage_plan(lat_parts, lon_parts, True)
    lon_plan = stage_plan(lat_parts, lon_parts, False)
    first_part = tile_count // (2 * parts) * parts
    live = []

    def start_sums(slot_of):
        spans = [(0, first_part), (first_part, tile_count - first_part)]
        for n, (start, length) in enumerate(spans):
            if length:
                steps = sum_steps(slot_of, start, length, 2 * slot_of + n, lon_plan if n == 0 else lat_plan)
                next(steps)
                live.append(steps)

    def tick(count=1):
        for _ in range(count):
            if live:
                steps = live.pop(0)
                if next(steps, "end") != "end":
                    live.append(steps)

    shift_grad(pad_g1, 0)
    kernel_terms(pad_a1, 0)
    start_sums(0)

    turn_act(pad_a2)
    halo_finish(halo_a2, pad_a2, 2)
    turn_halo(pad_a2)
    tick(2)
    kernel_terms(pad_a2, 1, tick)
    start_sums(1)
    halo_finish(halo_g1, pad_g1, 3)

    def last_grad(h, total):
        g = pad_g1[h + 2, 0:cols].astype(F32) + slope1[h] * total
        back2[h] = g

    conv(pad_g1, 1, last_grad, lambda: tick(2))
    grads = jnp.dot(
        featx[...], back2[...].astype(BF16).reshape(rows * cols, channels), preferred_element_type=F32
    )
    small[0] = grads[0 : small.shape[1]].astype(BF16)
    sum_c = small_steps(lat_plan)
    next(sum_c)
    live.insert(0, sum_c)

    def last_layer(h, total):
        enc_ref[h] = (x_keep[h] + total).astype(BF16)

    conv(pad_a2, 2, last_layer, lambda: tick(3))
    while live:
        tick()

    for copies in (halo_g2, halo_a1, halo_a2, halo_g1):
        halo_drain(copies)

    @pl.loop(1, parts)
    def _(dist):
        for copy in row_copies(dist):
            copy.wait_send()


def widen(scale, enc_in, kgrad_in, small_in, enc_out, kgrad_out, obs_out, field_out):
    enc_out[...] = enc_in[...]
    kgrad_out[...] = scale * kgrad_in[...].astype(F32)
    wide = scale * small_in[...].astype(F32)
    obs_out[...] = wide[: obs_out.shape[0]]
    field_out[...] = wide[obs_out.shape[0] : obs_out.shape[0] + field_out.shape[0]]


def per_device(
    grid_fields, obs_values, obs_count, obs_cell, obs_valid, obs_dist2,
    field_weight, obs_weight, conv_kernel, cotangent,
):
    rows, cols, channels = cotangent.shape
    lat_parts = lax.axis_size("lat")
    lon_parts = lax.axis_size("lon")
    parts = lat_parts * lon_parts
    fields = grid_fields.shape[0]
    width = obs_values.shape[3]
    capacity = obs_values.shape[2]
    wide = cols + SIDE
    tiles = TAPS * TAPS * channels // 16
    tiles = -(-tiles // parts) * parts
    plan = stage_plan(lat_parts, lon_parts, True)
    hops = sum(stage[1] - 1 for stage in plan)
    deep = -(-(width + fields) // 128) * 128
    small_rows = -(-(width + fields) // 16) * 16
    vmem = pl.BlockSpec(memory_space=pltpu.VMEM)
    pads = [pltpu.VMEM((rows + 4, wide, channels), BF16)] * 4
    encoded, kgrad, small = pl.pallas_call(
        functools.partial(kernel, lat_parts, lon_parts),
        out_shape=(
            jax.ShapeDtypeStruct((rows, cols, channels), BF16),
            jax.ShapeDtypeStruct((2, tiles, 16, channels), BF16),
            jax.ShapeDtypeStruct((small_rows, channels), BF16),
        ),
        in_specs=[vmem] * 10,
        out_specs=(vmem, vmem, vmem),
        scratch_shapes=[
            pltpu.VMEM((parts, 2, 128), F32),
            pltpu.VMEM((parts, capacity, width), BF16),
            pltpu.VMEM((parts, 2, 128), F32),
            pltpu.VMEM((deep, rows * cols), BF16),
            pltpu.VMEM((deep, channels), BF16),
            pltpu.VMEM((4, TAPS * channels, TAPS * channels), BF16),
            *pads,
            pltpu.VMEM((4, 4, SIDE, channels), BF16),
            pltpu.VMEM((4, 4, SIDE, channels), BF16),
            pltpu.VMEM((4, 2, 2, rows, channels), BF16),
            pltpu.VMEM((4, 2, 2, rows, channels), BF16),
            pltpu.VMEM((rows * SIDE, channels), F32),
            pltpu.VMEM((rows * SIDE, channels), F32),
            pltpu.VMEM((rows * SIDE, channels), F32),
            pltpu.VMEM((fields * rows, cols), F32),
            pltpu.VMEM((rows + 4, channels, cols), BF16),
            pltpu.VMEM((2, rows, cols, TAPS * channels), BF16),
            pltpu.VMEM((2, rows, SIDE, TAPS * channels), BF16),
            pltpu.VMEM((rows, cols, channels), F32),
            pltpu.VMEM((rows, cols, channels), F32),
            pltpu.VMEM((rows, cols, channels), F32),
            pltpu.VMEM((TAPS * channels, TAPS * channels), F32),
            pltpu.VMEM((2, tiles, 16, channels), BF16),
            pltpu.VMEM((2, tiles, 16, channels), BF16),
            pltpu.VMEM((2, tiles, 16, channels), BF16),
            pltpu.VMEM((len(plan) + 1, small_rows, channels), BF16),
            pltpu.VMEM((hops, small_rows, channels), BF16),
            pltpu.SemaphoreType.DMA((2, parts)),
            pltpu.SemaphoreType.DMA((2, parts)),
            pltpu.SemaphoreType.DMA((2,)),
            pltpu.SemaphoreType.DMA((4, 8)),
            pltpu.SemaphoreType.DMA((4, 8)),
            pltpu.SemaphoreType.DMA((4, hops)),
            pltpu.SemaphoreType.DMA((4, hops)),
            pltpu.SemaphoreType.DMA((4, hops)),
            pltpu.SemaphoreType.DMA((4, hops)),
            pltpu.SemaphoreType.DMA((hops,)),
            pltpu.SemaphoreType.DMA((hops,)),
        ],
        compiler_params=pltpu.CompilerParams(
            collective_id=0, has_side_effects=True, vmem_limit_bytes=56 * 1024 * 1024
        ),
        name="encoder",
    )(
        grid_fields, obs_values, obs_count, jnp.swapaxes(obs_cell, 1, 2),
        jnp.swapaxes(obs_valid, 1, 2), jnp.swapaxes(obs_dist2, 1, 2),
        field_weight, obs_weight, conv_kernel, cotangent,
    )
    scale = 1.0 / (rows * lat_parts * cols * lon_parts) ** 0.5
    used = TAPS * TAPS * channels // 16
    steps = math.gcd(math.gcd(used, rows), 4)
    encoded, kernel_grad, obs_grad, field_grad = pl.pallas_call(
        functools.partial(widen, scale),
        grid=(steps,),
        in_specs=[
            pl.BlockSpec((rows // steps, cols, channels), lambda n: (n, 0, 0)),
            pl.BlockSpec((2, used // steps, 16, channels), lambda n: (0, n, 0, 0)),
            pl.BlockSpec((small_rows, channels), lambda n: (0, 0)),
        ],
        out_specs=[
            pl.BlockSpec((rows // steps, cols, channels), lambda n: (n, 0, 0)),
            pl.BlockSpec((2, used // steps, 16, channels), lambda n: (0, n, 0, 0)),
            pl.BlockSpec((width, channels), lambda n: (0, 0)),
            pl.BlockSpec((fields, channels), lambda n: (0, 0)),
        ],
        out_shape=(
            jax.ShapeDtypeStruct((rows, cols, channels), BF16),
            jax.ShapeDtypeStruct((2, used, 16, channels), F32),
            jax.ShapeDtypeStruct((width, channels), F32),
            jax.ShapeDtypeStruct((fields, channels), F32),
        ),
        name="widen",
    )(encoded, kgrad, small)
    return encoded, kernel_grad.reshape(2, TAPS, TAPS, channels, channels), obs_grad, field_grad


def solution(mesh):
    return jax.shard_map(
        per_device,
        mesh=mesh,
        in_specs=(
            P(None, "lat", "lon"),
            P(("lat", "lon"), None, None, None),
            P(("lat", "lon"), None),
            P(("lat", "lon"), None, None),
            P(("lat", "lon"), None, None),
            P(("lat", "lon"), None, None),
            P(),
            P(),
            P(),
            P("lat", "lon", None),
        ),
        out_specs=(P("lat", "lon", None), P(), P(), P()),
        check_vma=False,
    )
```

```python
import functools
import math

import jax
import jax.numpy as jnp
from jax import lax
from jax.experimental import pallas as pl
from jax.experimental.pallas import tpu as pltpu
from jax.sharding import PartitionSpec as P

BF16 = jnp.bfloat16
F32 = jnp.float32
MESH = pl.DeviceIdType.MESH
TAPS = 5
SIDE = 16
ROOT = 0.7978845608028654


def gelu_pair(x):
    cubic = 0.044715 * x * x
    bend = jnp.tanh(ROOT * x * (1.0 + cubic))
    half = 0.5 * (1.0 + bend)
    slope = half + 0.5 * x * (1.0 - bend * bend) * (ROOT * (1.0 + 3.0 * cubic))
    return x * half, slope


def stage_plan(lat_parts, lon_parts, lat_first):
    lat = [("lat", 2, 1), ("lat", lat_parts // 2, 2)] if lat_parts % 2 == 0 else [("lat", lat_parts, 1)]
    lon = [("lon", 2, 1), ("lon", lon_parts // 2, 2)] if lon_parts % 2 == 0 else [("lon", lon_parts, 1)]
    if lat_first:
        plan = lat + lon
    else:
        plan = lat[:1] + lon[:1] + lat[1:] + lon[1:]
    return [stage for stage in plan if stage[1] > 1]


class Group:
    def __init__(self, stage, lat, lon):
        self.axis, self.size, self.stride = stage
        self.lat, self.lon = lat, lon
        pos = lat if self.axis == "lat" else lon
        self.rank = lax.rem(pos // self.stride, self.size)
        self.pos = pos

    def rank_at(self, dist):
        return lax.rem(self.rank + dist, self.size)

    def device(self, rank):
        pos = self.pos + (rank - self.rank) * self.stride
        return (pos, self.lon) if self.axis == "lat" else (self.lat, pos)


def kernel(
    lat_parts, lon_parts,
    fields_ref, values_ref, count_ref, cell_ref, valid_ref, dist_ref,
    field_w_ref, obs_w_ref, conv_ref, cot_ref,
    enc_ref, kgrad_ref, small_ref,
    header, vrecv, hrecv, featx, wcat, wbuf, pad_g2, pad_a1, pad_a2, pad_g1,
    left, right, strip_out, strip_in, strip_w, strip_e, strip_z, field_rows,
    turned, shifted, shifted_side, back2, x_keep, slope1,
    kacc, part, final, inbox, small, small_in,
    a2a_send, a2a_recv, own_sem, halo_send, halo_recv,
    rs_send, rs_recv, ag_send, ag_recv, sm_send, sm_recv,
):
    lat = lax.axis_index("lat")
    lon = lax.axis_index("lon")
    parts = lat_parts * lon_parts
    me = lat * lon_parts + lon
    rows, cols, channels = cot_ref.shape
    capacity = values_ref.shape[2]
    side = slice(cols, cols + SIDE)
    wide = cols + SIDE
    tile_count = part.shape[1]

    def device_at(dist):
        peer = lax.rem(me + dist, parts)
        return peer, (peer // lon_parts, lax.rem(peer, lon_parts))

    barrier = pltpu.get_barrier_semaphore()

    @pl.loop(1, parts)
    def _(dist):
        pl.semaphore_signal(barrier, inc=1, device_id=device_at(dist)[1], device_id_type=MESH)

    slot = lax.broadcasted_iota(jnp.int32, (capacity, parts), 0)
    used = (valid_ref[0] == 1) & (slot < count_ref[...])
    weight = jnp.where(used, jnp.exp(-0.5 * dist_ref[0]), 0.0).astype(BF16).astype(F32)
    header[...] = jnp.zeros_like(header)
    header[:, 0, 0:capacity] = weight.T
    header[:, 1, 0:capacity] = cell_ref[0].astype(F32).T

    def clear_edges(pad, k):
        zero = jnp.zeros((2, wide, channels), BF16)
        zero_side = jnp.zeros((2, SIDE, channels), BF16)

        @pl.when(lat == 0)
        def _():
            pad[0:2] = zero
            left[k, 0:2] = zero_side
            right[k, 0:2] = zero_side

        @pl.when(lat == lat_parts - 1)
        def _():
            pad[rows + 2 : rows + 4] = zero
            left[k, 2:4] = zero_side
            right[k, 2:4] = zero_side

    def halo_copies(pad, k):
        up, down = lat - 1, lat + 1
        west = lax.rem(lon + lon_parts - 1, lon_parts)
        east = lax.rem(lon + 1, lon_parts)
        first, last = slice(2, 4), slice(rows, rows + 2)
        above, below = slice(0, 2), slice(rows + 2, rows + 4)
        top, bottom = slice(0, 2), slice(2, 4)
        lo, hi, full = slice(0, SIDE), slice(cols - SIDE, cols), slice(0, cols)
        has_up, has_down = lat > 0, lat < lat_parts - 1
        table = [
            (pad.at[first, full], pad.at[below, full], (up, lon), has_up, has_down),
            (pad.at[last, full], pad.at[above, full], (down, lon), has_down, has_up),
            (strip_out.at[k, 0], strip_in.at[k, 0], (lat, west), None, None),
            (strip_out.at[k, 1], strip_in.at[k, 1], (lat, east), None, None),
            (pad.at[first, lo], right.at[k, bottom], (up, west), has_up, has_down),
            (pad.at[first, hi], left.at[k, bottom], (up, east), has_up, has_down),
            (pad.at[last, lo], right.at[k, top], (down, west), has_down, has_up),
            (pad.at[last, hi], left.at[k, top], (down, east), has_down, has_up),
        ]
        out = []
        for n, (src, dst, dev, can_send, can_recv) in enumerate(table):
            copy = pltpu.make_async_remote_copy(
                src_ref=src, dst_ref=dst, send_sem=halo_send.at[k, n], recv_sem=halo_recv.at[k, n],
                device_id=dev, device_id_type=MESH,
            )
            out.append((copy, can_send, can_recv))
        return out

    def guarded(cond, act):
        if cond is None:
            act()
        else:
            pl.when(cond)(act)

    def halo_start(copies, pad, k):
        for copy, can_send, _ in copies[:2]:
            guarded(can_send, copy.start)
        for copy, can_send, _ in copies[4:]:
            guarded(can_send, copy.start)
        strip_w[...] = pad[2 : rows + 2, 0:SIDE].reshape(rows * SIDE, channels).astype(F32)
        strip_e[...] = (
            pad[2 : rows + 2, cols - SIDE : cols].reshape(rows * SIDE, channels).astype(F32)
        )
        for j in range(2):
            strip_out[k, 0, j] = strip_w[pl.ds(j, rows, stride=SIDE)].astype(BF16)
            strip_out[k, 1, j] = strip_e[pl.ds(SIDE - 2 + j, rows, stride=SIDE)].astype(BF16)
        for copy, can_send, _ in copies[2:4]:
            guarded(can_send, copy.start)

    def halo_finish(copies, pad, k):
        for copy, _, can_recv in copies:
            guarded(can_recv, copy.wait_recv)
        for j in range(2):
            strip_z[pl.ds(j, rows, stride=SIDE)] = strip_in[k, 0, j].astype(F32)
            strip_z[pl.ds(SIDE - 2 + j, rows, stride=SIDE)] = strip_in[k, 1, j].astype(F32)
        pad[2 : rows + 2, side] = strip_z[...].astype(BF16).reshape(rows, SIDE, channels)
        at = lax.broadcasted_iota(jnp.int32, (4, SIDE, channels), 1)
        corner = jnp.where(
            at < 2, right[k].astype(F32), jnp.where(at >= SIDE - 2, left[k].astype(F32), 0.0)
        ).astype(BF16)
        pad[0:2, side] = corner[0:2]
        pad[rows + 2 : rows + 4, side] = corner[2:4]

    def halo_drain(copies):
        for copy, can_send, _ in copies:
            guarded(can_send, copy.wait_send)

    def place_weights(layer, turn):
        at = 2 * layer + turn
        for p in range(TAPS):
            for q in range(TAPS):
                if turn:
                    block = conv_ref[layer, TAPS - 1 - p, TAPS - 1 - q].T
                else:
                    block = conv_ref[layer, p, q]
                wbuf[at, p * channels : (p + 1) * channels, q * channels : (q + 1) * channels] = block

    group = 4 if rows % 4 == 0 else 1

    def conv(pad, at, finish, between=None):
        def one(b):
            lhs = jnp.concatenate(
                [pad[pl.ds(b * group + p, group)].reshape(group * wide, channels) for p in range(TAPS)],
                axis=1,
            )
            prod = jnp.dot(lhs, wbuf[at], preferred_element_type=F32)
            for r in range(group):
                total = None
                for q in range(TAPS):
                    piece = prod[r * wide : (r + 1) * wide, q * channels : (q + 1) * channels]
                    shift = (2 - q) % wide
                    if shift:
                        piece = pltpu.roll(piece, shift, 0)
                    piece = piece[:cols]
                    total = piece if total is None else total + piece
                finish(b * group + r, total)

        if between is None:
            pl.loop(0, rows // group)(one)
        else:
            for b in range(rows // group):
                one(b)
                between()

    def shift_grad(pad, at):
        @pl.loop(0, rows // group)
        def _(b):
            for r in range(group):
                h = b * group + r
                ext = jnp.concatenate(
                    [pad[h + 2, 0:cols].astype(F32), jnp.zeros((SIDE, channels), F32)], axis=0
                )
                for q in range(TAPS):
                    shift = (q - 2) % wide
                    moved = (pltpu.roll(ext, shift, 0) if shift else ext).astype(BF16)
                    lanes = slice(q * channels, (q + 1) * channels)
                    shifted[at, h, :, lanes] = moved[:cols]
                    shifted_side[at, h, :, lanes] = moved[cols:]

    def turn_act(pad):
        @pl.loop(0, rows // group)
        def _(b):
            for r in range(group):
                h = b * group + r + 2
                turned[h] = pad[h, 0:cols].T

    def turn_halo(pad):
        for h in (0, 1, rows + 2, rows + 3):
            turned[h] = pad[h, 0:cols].T

    def kernel_terms(pad, slot_of, between=None):
        side_lhs = jnp.concatenate(
            [pad[p : p + rows, side].reshape(rows * SIDE, channels).T for p in range(TAPS)], axis=0
        )
        kacc[...] = jnp.dot(
            side_lhs, shifted_side[slot_of].reshape(rows * SIDE, TAPS * channels),
            preferred_element_type=F32,
        )

        def one(b):
            lhs = jnp.concatenate(
                [
                    jnp.concatenate([turned[b * group + p + r] for r in range(group)], axis=1)
                    for p in range(TAPS)
                ],
                axis=0,
            )
            rhs = shifted[slot_of, pl.ds(b * group, group)].reshape(group * cols, TAPS * channels)
            kacc[...] += jnp.dot(lhs, rhs, preferred_element_type=F32)

        if between is None:
            pl.loop(0, rows // group)(one)
        else:
            for b in range(rows // group):
                one(b)
                between()
        per = channels // 16
        for p in range(TAPS):
            for q in range(TAPS):
                block = kacc[p * channels : (p + 1) * channels, q * channels : (q + 1) * channels]
                n = (p * TAPS + q) * per
                part[slot_of, n : n + per] = block.astype(BF16).reshape(per, 16, channels)
        used_tiles = TAPS * TAPS * per
        if used_tiles < tile_count:
            part[slot_of, used_tiles:] = jnp.zeros(
                (tile_count - used_tiles, 16, channels), BF16
            )

    def sum_steps(slot_of, start, length, stream, plan):
        groups = [Group(stage, lat, lon) for stage in plan]
        pending = []
        base = start
        box = start
        whole = slice(start, start + length)
        nsem = 0
        bases = []
        for g in groups:
            share = length // g.size
            sent = []
            for dist in range(1, g.size):
                copy = pltpu.make_async_remote_copy(
                    src_ref=part.at[slot_of, pl.ds(base + g.rank_at(dist) * share, share)],
                    dst_ref=inbox.at[slot_of, pl.ds(box + (dist - 1) * share, share)],
                    send_sem=rs_send.at[stream, nsem], recv_sem=rs_recv.at[stream, nsem],
                    device_id=g.device(g.rank_at(dist)), device_id_type=MESH,
                )
                copy.start()
                sent.append(copy)
                nsem += 1
            pending += sent
            yield
            for copy in sent:
                copy.wait_recv()
            mine = base + g.rank * share
            total = part[slot_of, pl.ds(mine, share)].astype(F32)
            for dist in range(1, g.size):
                at = box + (dist - 1) * share
                total = total + inbox[slot_of, at : at + share].astype(F32)
            part[slot_of, pl.ds(mine, share)] = total.astype(BF16)
            box += (g.size - 1) * share
            bases.append(base)
            base, length = mine, share
        final[slot_of, pl.ds(base, length)] = part[slot_of, pl.ds(base, length)]
        nsem = 0
        for g, low in zip(reversed(groups), reversed(bases)):
            sent, got = [], []
            for dist in range(1, g.size):
                copy = pltpu.make_async_remote_copy(
                    src_ref=final.at[slot_of, pl.ds(base, length)],
                    dst_ref=final.at[slot_of, pl.ds(base, length)],
                    send_sem=ag_send.at[stream, nsem], recv_sem=ag_recv.at[stream, nsem],
                    device_id=g.device(g.rank_at(dist)), device_id_type=MESH,
                )
                copy.start()
                sent.append(copy)
                here = final.at[slot_of, pl.ds(low + g.rank_at(g.size - dist) * length, length)]
                got.append(
                    pltpu.make_async_remote_copy(
                        src_ref=here, dst_ref=here,
                        send_sem=ag_send.at[stream, nsem], recv_sem=ag_recv.at[stream, nsem],
                        device_id=g.device(g.rank_at(dist)), device_id_type=MESH,
                    )
                )
                nsem += 1
            pending += sent
            yield
            for copy in got:
                copy.wait_recv()
            base, length = low, length * g.size
        for copy in pending:
            copy.wait_send()
        kgrad_ref[slot_of, whole] = final[slot_of, whole]

    def small_steps(plan):
        nsem = 0
        pending = []
        for n, stage in enumerate(plan):
            g = Group(stage, lat, lon)
            sent = []
            for dist in range(1, g.size):
                copy = pltpu.make_async_remote_copy(
                    src_ref=small.at[n], dst_ref=small_in.at[nsem],
                    send_sem=sm_send.at[nsem], recv_sem=sm_recv.at[nsem],
                    device_id=g.device(g.rank_at(dist)), device_id_type=MESH,
                )
                copy.start()
                sent.append((copy, nsem, dist))
                nsem += 1
            pending += sent
            yield
            for copy, _, _ in sent:
                copy.wait_recv()
            total = jnp.zeros(small.shape[1:], F32)
            mine = small[n].astype(F32)
            for rank in range(g.size):
                term = mine
                for _, box, dist in sent:
                    term = jnp.where(g.rank_at(g.size - dist) == rank, small_in[box].astype(F32), term)
                total = total + term
            small[n + 1] = total.astype(BF16)
        for copy, _, _ in pending:
            copy.wait_send()
        small_ref[...] = small[len(plan)]

    pad_g2[2 : rows + 2, 0:cols] = cot_ref[...]
    for k, pad in enumerate((pad_g2, pad_a1, pad_a2, pad_g1)):
        clear_edges(pad, k)
    strip_z[...] = jnp.zeros_like(strip_z)
    place_weights(1, True)
    field_count = fields_ref.shape[0]
    width = values_ref.shape[3]
    featx[width:, :] = jnp.zeros((featx.shape[0] - width, featx.shape[1]), BF16)
    field_rows[...] = fields_ref[...].astype(F32).reshape(field_count * rows, cols)
    for h in range(rows):
        featx[width : width + field_count, h * cols : (h + 1) * cols] = field_rows[
            pl.ds(h, field_count, stride=rows)
        ].astype(BF16)
    wcat[...] = jnp.zeros_like(wcat)
    wcat[0:width] = obs_w_ref[...]
    wcat[width : width + field_count] = field_w_ref[...]

    pl.semaphore_wait(barrier, parts - 1)

    own = pltpu.make_async_copy(values_ref.at[0, me], vrecv.at[me], own_sem.at[0])
    own.start()
    own_head = pltpu.make_async_copy(header.at[me], hrecv.at[me], own_sem.at[1])
    own_head.start()

    def row_copies(dist):
        peer, dev = device_at(dist)
        return [
            pltpu.make_async_remote_copy(
                src_ref=src, dst_ref=dst, send_sem=a2a_send.at[n, dist], recv_sem=a2a_recv.at[n, dist],
                device_id=dev, device_id_type=MESH,
            )
            for n, (src, dst) in enumerate(
                ((values_ref.at[0, peer], vrecv.at[me]), (header.at[peer], hrecv.at[me]))
            )
        ]

    @pl.loop(1, parts)
    def _(dist):
        for copy in row_copies(dist):
            copy.start()

    halo_g2 = halo_copies(pad_g2, 0)
    halo_start(halo_g2, pad_g2, 0)
    shift_grad(pad_g2, 1)
    place_weights(0, False)
    halo_finish(halo_g2, pad_g2, 0)

    def keep_back(h, total):
        back2[h] = total

    conv(pad_g2, 3, keep_back)

    own.wait()
    own_head.wait()

    @pl.loop(1, parts)
    def _(dist):
        sender = lax.rem(me + parts - dist, parts)
        for n, dst in enumerate((vrecv.at[sender], hrecv.at[sender])):
            pltpu.make_async_remote_copy(
                src_ref=dst, dst_ref=dst, send_sem=a2a_send.at[n, dist], recv_sem=a2a_recv.at[n, dist],
                device_id=device_at(dist)[1], device_id_type=MESH,
            ).wait_recv()

    count = parts * capacity
    lane = lax.broadcasted_iota(jnp.int32, (count, 128), 1)
    pick = lane == lax.rem(lax.broadcasted_iota(jnp.int32, (count, 128), 0), capacity)

    def column(n):
        spread = jnp.broadcast_to(hrecv[:, n : n + 1, :], (parts, capacity, 128)).reshape(count, 128)
        return jnp.sum(jnp.where(pick, spread, 0.0), axis=1, keepdims=True)

    w_col, cell_col = column(0), column(1)
    values_t = jnp.concatenate(
        [vrecv[...].reshape(count, width).T, jnp.ones((16, count), BF16)], axis=0
    )
    block = 512 if (rows * cols) % 512 == 0 else cols

    @pl.loop(0, rows * cols // block)
    def _(b):
        start = pl.multiple_of(b * block, block)
        ids = (start + lax.broadcasted_iota(jnp.int32, (count, block), 1)).astype(F32)
        spread = jnp.where(ids == cell_col, w_col, 0.0).astype(BF16)
        sums = jnp.dot(values_t, spread, preferred_element_type=F32)
        dens = sums[width : width + 1]
        featx[0:width, pl.ds(start, block)] = (sums[0:width] / (1.0 + dens)).astype(BF16)

    @pl.loop(0, rows // group)
    def _(b):
        start = pl.multiple_of(b * group * cols, group * cols)
        feats = featx[:, pl.ds(start, group * cols)].T
        x = jnp.dot(feats, wcat[...], preferred_element_type=F32).astype(BF16).astype(F32)
        x = x.reshape(group, cols, channels)
        act, slope = gelu_pair(x)
        at = pl.ds(b * group, group)
        x_keep[at] = x
        slope1[at] = slope
        pad_a1[pl.ds(b * group + 2, group), 0:cols] = act.astype(BF16)

    halo_a1 = halo_copies(pad_a1, 1)
    halo_start(halo_a1, pad_a1, 1)
    turn_act(pad_a1)
    halo_finish(halo_a1, pad_a1, 1)
    turn_halo(pad_a1)

    def first_layer(h, total):
        x = (x_keep[h] + total).astype(BF16).astype(F32)
        act, slope = gelu_pair(x)
        x_keep[h] = x
        pad_a2[h + 2, 0:cols] = act.astype(BF16)
        g = cot_ref[h].astype(F32) + slope * back2[h]
        pad_g1[h + 2, 0:cols] = g.astype(BF16)

    conv(pad_a1, 0, first_layer)
    halo_a2 = halo_copies(pad_a2, 2)
    halo_start(halo_a2, pad_a2, 2)
    halo_g1 = halo_copies(pad_g1, 3)
    halo_start(halo_g1, pad_g1, 3)

    lat_plan = stage_plan(lat_parts, lon_parts, True)
    lon_plan = stage_plan(lat_parts, lon_parts, False)
    first_part = tile_count // (2 * parts) * parts
    live = []

    def start_sums(slot_of):
        spans = [(0, first_part), (first_part, tile_count - first_part)]
        for n, (start, length) in enumerate(spans):
            if length:
                steps = sum_steps(slot_of, start, length, 2 * slot_of + n, lon_plan if n == 0 else lat_plan)
                next(steps)
                live.append(steps)

    def tick(count=1):
        for _ in range(count):
            if live:
                steps = live.pop(0)
                if next(steps, "end") != "end":
                    live.append(steps)

    shift_grad(pad_g1, 0)
    kernel_terms(pad_a1, 0)
    start_sums(0)

    turn_act(pad_a2)
    halo_finish(halo_a2, pad_a2, 2)
    turn_halo(pad_a2)
    tick(2)
    kernel_terms(pad_a2, 1, tick)
    start_sums(1)
    place_weights(0, True)
    halo_finish(halo_g1, pad_g1, 3)
    tick(2)

    def last_grad(h, total):
        g = pad_g1[h + 2, 0:cols].astype(F32) + slope1[h] * total
        back2[h] = g

    conv(pad_g1, 1, last_grad, lambda: tick(2))
    grads = jnp.dot(
        featx[...], back2[...].astype(BF16).reshape(rows * cols, channels), preferred_element_type=F32
    )
    small[0] = grads[0 : small.shape[1]].astype(BF16)
    sum_c = small_steps(lat_plan)
    next(sum_c)
    live.insert(0, sum_c)

    place_weights(1, False)

    def last_layer(h, total):
        enc_ref[h] = (x_keep[h] + total).astype(BF16)

    conv(pad_a2, 2, last_layer, lambda: tick(3))
    while live:
        tick()

    for copies in (halo_g2, halo_a1, halo_a2, halo_g1):
        halo_drain(copies)

    @pl.loop(1, parts)
    def _(dist):
        for copy in row_copies(dist):
            copy.wait_send()


def widen(scale, chunks, enc_in, kgrad_in, small_in, enc_out, kgrad_out, obs_out, field_out, stage, sems):
    copies = [pltpu.make_async_copy(enc_in, enc_out, sems.at[2 * chunks])]
    copies[0].start()
    per = stage.shape[1] // chunks
    for n in range(2 * chunks):
        at = (n // chunks, slice(n % chunks * per, (n % chunks + 1) * per))
        stage[at] = scale * kgrad_in[at].astype(F32)
        copies.append(pltpu.make_async_copy(stage.at[at], kgrad_out.at[at], sems.at[n]))
        copies[-1].start()
    wide = scale * small_in[...].astype(F32)
    obs_out[...] = wide[: obs_out.shape[0]]
    field_out[...] = wide[obs_out.shape[0] : obs_out.shape[0] + field_out.shape[0]]
    for copy in copies:
        copy.wait()


def per_device(
    grid_fields, obs_values, obs_count, obs_cell, obs_valid, obs_dist2,
    field_weight, obs_weight, conv_kernel, cotangent,
):
    rows, cols, channels = cotangent.shape
    lat_parts = lax.axis_size("lat")
    lon_parts = lax.axis_size("lon")
    parts = lat_parts * lon_parts
    fields = grid_fields.shape[0]
    width = obs_values.shape[3]
    capacity = obs_values.shape[2]
    wide = cols + SIDE
    tiles = TAPS * TAPS * channels // 16
    tiles = -(-tiles // parts) * parts
    plan = stage_plan(lat_parts, lon_parts, True)
    hops = sum(stage[1] - 1 for stage in plan)
    deep = -(-(width + fields) // 128) * 128
    small_rows = -(-(width + fields) // 16) * 16
    vmem = pl.BlockSpec(memory_space=pltpu.VMEM)
    pads = [pltpu.VMEM((rows + 4, wide, channels), BF16)] * 4
    encoded, kgrad, small = pl.pallas_call(
        functools.partial(kernel, lat_parts, lon_parts),
        out_shape=(
            jax.ShapeDtypeStruct((rows, cols, channels), BF16),
            jax.ShapeDtypeStruct((2, tiles, 16, channels), BF16),
            jax.ShapeDtypeStruct((small_rows, channels), BF16),
        ),
        in_specs=[vmem] * 10,
        out_specs=(vmem, vmem, vmem),
        scratch_shapes=[
            pltpu.VMEM((parts, 2, 128), F32),
            pltpu.VMEM((parts, capacity, width), BF16),
            pltpu.VMEM((parts, 2, 128), F32),
            pltpu.VMEM((deep, rows * cols), BF16),
            pltpu.VMEM((deep, channels), BF16),
            pltpu.VMEM((4, TAPS * channels, TAPS * channels), BF16),
            *pads,
            pltpu.VMEM((4, 4, SIDE, channels), BF16),
            pltpu.VMEM((4, 4, SIDE, channels), BF16),
            pltpu.VMEM((4, 2, 2, rows, channels), BF16),
            pltpu.VMEM((4, 2, 2, rows, channels), BF16),
            pltpu.VMEM((rows * SIDE, channels), F32),
            pltpu.VMEM((rows * SIDE, channels), F32),
            pltpu.VMEM((rows * SIDE, channels), F32),
            pltpu.VMEM((fields * rows, cols), F32),
            pltpu.VMEM((rows + 4, channels, cols), BF16),
            pltpu.VMEM((2, rows, cols, TAPS * channels), BF16),
            pltpu.VMEM((2, rows, SIDE, TAPS * channels), BF16),
            pltpu.VMEM((rows, cols, channels), F32),
            pltpu.VMEM((rows, cols, channels), F32),
            pltpu.VMEM((rows, cols, channels), F32),
            pltpu.VMEM((TAPS * channels, TAPS * channels), F32),
            pltpu.VMEM((2, tiles, 16, channels), BF16),
            pltpu.VMEM((2, tiles, 16, channels), BF16),
            pltpu.VMEM((2, tiles, 16, channels), BF16),
            pltpu.VMEM((len(plan) + 1, small_rows, channels), BF16),
            pltpu.VMEM((hops, small_rows, channels), BF16),
            pltpu.SemaphoreType.DMA((2, parts)),
            pltpu.SemaphoreType.DMA((2, parts)),
            pltpu.SemaphoreType.DMA((2,)),
            pltpu.SemaphoreType.DMA((4, 8)),
            pltpu.SemaphoreType.DMA((4, 8)),
            pltpu.SemaphoreType.DMA((4, hops)),
            pltpu.SemaphoreType.DMA((4, hops)),
            pltpu.SemaphoreType.DMA((4, hops)),
            pltpu.SemaphoreType.DMA((4, hops)),
            pltpu.SemaphoreType.DMA((hops,)),
            pltpu.SemaphoreType.DMA((hops,)),
        ],
        compiler_params=pltpu.CompilerParams(
            collective_id=0, has_side_effects=True, vmem_limit_bytes=56 * 1024 * 1024
        ),
        name="encoder",
    )(
        grid_fields, obs_values, obs_count, jnp.swapaxes(obs_cell, 1, 2),
        jnp.swapaxes(obs_valid, 1, 2), jnp.swapaxes(obs_dist2, 1, 2),
        field_weight, obs_weight, conv_kernel, cotangent,
    )
    scale = 1.0 / (rows * lat_parts * cols * lon_parts) ** 0.5
    used = TAPS * TAPS * channels // 16
    chunks = math.gcd(used, 4)
    encoded, kernel_grad, obs_grad, field_grad = pl.pallas_call(
        functools.partial(widen, scale, chunks),
        in_specs=[vmem] * 3,
        out_specs=[pl.BlockSpec(memory_space=pl.ANY)] * 2 + [vmem] * 2,
        out_shape=(
            jax.ShapeDtypeStruct((rows, cols, channels), BF16),
            jax.ShapeDtypeStruct((2, used, 16, channels), F32),
            jax.ShapeDtypeStruct((width, channels), F32),
            jax.ShapeDtypeStruct((fields, channels), F32),
        ),
        scratch_shapes=[
            pltpu.VMEM((2, used, 16, channels), F32),
            pltpu.SemaphoreType.DMA((2 * chunks + 1,)),
        ],
        compiler_params=pltpu.CompilerParams(vmem_limit_bytes=32 * 1024 * 1024),
        name="widen",
    )(encoded, kgrad, small)
    return encoded, kernel_grad.reshape(2, TAPS, TAPS, channels, channels), obs_grad, field_grad


def solution(mesh):
    return jax.shard_map(
        per_device,
        mesh=mesh,
        in_specs=(
            P(None, "lat", "lon"),
            P(("lat", "lon"), None, None, None),
            P(("lat", "lon"), None),
            P(("lat", "lon"), None, None),
            P(("lat", "lon"), None, None),
            P(("lat", "lon"), None, None),
            P(),
            P(),
            P(),
            P("lat", "lon", None),
        ),
        out_specs=(P("lat", "lon", None), P(), P(), P()),
        check_vma=False,
    )
```

```python
import functools
import math

import jax
import jax.numpy as jnp
from jax import lax
from jax.experimental import pallas as pl
from jax.experimental.pallas import tpu as pltpu
from jax.sharding import PartitionSpec as P

BF16 = jnp.bfloat16
F32 = jnp.float32
MESH = pl.DeviceIdType.MESH
TAPS = 5
SIDE = 16
ROOT = 0.7978845608028654


def gelu_pair(x):
    cubic = 0.044715 * x * x
    bend = jnp.tanh(ROOT * x * (1.0 + cubic))
    half = 0.5 * (1.0 + bend)
    slope = half + 0.5 * x * (1.0 - bend * bend) * (ROOT * (1.0 + 3.0 * cubic))
    return x * half, slope


def stage_plan(lat_parts, lon_parts, lat_first):
    lat = [("lat", 2, 1), ("lat", lat_parts // 2, 2)] if lat_parts % 2 == 0 else [("lat", lat_parts, 1)]
    lon = [("lon", 2, 1), ("lon", lon_parts // 2, 2)] if lon_parts % 2 == 0 else [("lon", lon_parts, 1)]
    if lat_first:
        plan = lat + lon
    else:
        plan = lat[:1] + lon[:1] + lat[1:] + lon[1:]
    return [stage for stage in plan if stage[1] > 1]


class Group:
    def __init__(self, stage, lat, lon):
        self.axis, self.size, self.stride = stage
        self.lat, self.lon = lat, lon
        pos = lat if self.axis == "lat" else lon
        self.rank = lax.rem(pos // self.stride, self.size)
        self.pos = pos

    def rank_at(self, dist):
        return lax.rem(self.rank + dist, self.size)

    def device(self, rank):
        pos = self.pos + (rank - self.rank) * self.stride
        return (pos, self.lon) if self.axis == "lat" else (self.lat, pos)


def kernel(
    lat_parts, lon_parts,
    fields_ref, values_ref, count_ref, cell_ref, valid_ref, dist_ref,
    field_w_ref, obs_w_ref, conv_ref, cot_ref,
    enc_ref, kgrad_ref, small_ref,
    header, outgoing, arrived, enc_keep, featx, wcat, wbuf, pad_g2, pad_a1, pad_a2, pad_g1,
    left, right, strip_out, strip_in, strip_w, strip_e, strip_z, field_rows,
    turned, shifted, shifted_side, back2, x_keep, slope1,
    kacc, part, final, inbox, small, small_in,
    a2a_send, a2a_recv, out_sem, halo_send, halo_recv,
    rs_send, rs_recv, ag_send, ag_recv, sm_send, sm_recv,
):
    lat = lax.axis_index("lat")
    lon = lax.axis_index("lon")
    parts = lat_parts * lon_parts
    me = lat * lon_parts + lon
    rows, cols, channels = cot_ref.shape
    capacity = values_ref.shape[2]
    side = slice(cols, cols + SIDE)
    wide = cols + SIDE
    tile_count = part.shape[1]

    def device_at(dist):
        peer = lax.rem(me + dist, parts)
        return peer, (lax.div(peer, lon_parts), lax.rem(peer, lon_parts))

    barrier = pltpu.get_barrier_semaphore()

    @pl.loop(1, parts)
    def _(dist):
        pl.semaphore_signal(barrier, inc=1, device_id=device_at(dist)[1], device_id_type=MESH)

    slot = lax.broadcasted_iota(jnp.int32, (capacity, parts), 0)
    used = (valid_ref[0] == 1) & (slot < count_ref[...])
    weight = jnp.where(used, jnp.exp(-0.5 * dist_ref[0]), 0.0).astype(BF16).astype(F32)
    header[...] = jnp.zeros_like(header)
    header[:, 0, 0:capacity] = weight.T
    cells = cell_ref[0].astype(F32)
    cell_row = jnp.floor(cells / cols)
    header[:, 1, 0:capacity] = cell_row.T
    header[:, 2, 0:capacity] = (cells - cell_row * cols).T
    line = lax.broadcasted_iota(jnp.int32, (parts, 16, 128), 1)
    head = jnp.zeros((parts, 16, 128), F32)
    for n in range(3):
        head = jnp.where(line == n, jnp.broadcast_to(header[:, n : n + 1, :], head.shape), head)
    outgoing[:, 0:capacity] = values_ref[0]
    outgoing[:, capacity:] = head.astype(BF16)

    def clear_edges(pad, k):
        zero = jnp.zeros((2, wide, channels), BF16)
        zero_side = jnp.zeros((2, SIDE, channels), BF16)

        @pl.when(lat == 0)
        def _():
            pad[0:2] = zero
            left[k, 0:2] = zero_side
            right[k, 0:2] = zero_side

        @pl.when(lat == lat_parts - 1)
        def _():
            pad[rows + 2 : rows + 4] = zero
            left[k, 2:4] = zero_side
            right[k, 2:4] = zero_side

    def halo_copies(pad, k):
        up, down = lat - 1, lat + 1
        west = lax.rem(lon + lon_parts - 1, lon_parts)
        east = lax.rem(lon + 1, lon_parts)
        first, last = slice(2, 4), slice(rows, rows + 2)
        above, below = slice(0, 2), slice(rows + 2, rows + 4)
        top, bottom = slice(0, 2), slice(2, 4)
        lo, hi, full = slice(0, SIDE), slice(cols - SIDE, cols), slice(0, cols)
        has_up, has_down = lat > 0, lat < lat_parts - 1
        table = [
            (pad.at[first, full], pad.at[below, full], (up, lon), has_up, has_down),
            (pad.at[last, full], pad.at[above, full], (down, lon), has_down, has_up),
            (strip_out.at[k, 0], strip_in.at[k, 0], (lat, west), None, None),
            (strip_out.at[k, 1], strip_in.at[k, 1], (lat, east), None, None),
            (pad.at[first, lo], right.at[k, bottom], (up, west), has_up, has_down),
            (pad.at[first, hi], left.at[k, bottom], (up, east), has_up, has_down),
            (pad.at[last, lo], right.at[k, top], (down, west), has_down, has_up),
            (pad.at[last, hi], left.at[k, top], (down, east), has_down, has_up),
        ]
        out = []
        for n, (src, dst, dev, can_send, can_recv) in enumerate(table):
            copy = pltpu.make_async_remote_copy(
                src_ref=src, dst_ref=dst, send_sem=halo_send.at[k, n], recv_sem=halo_recv.at[k, n],
                device_id=dev, device_id_type=MESH,
            )
            out.append((copy, can_send, can_recv))
        return out

    def guarded(cond, act):
        if cond is None:
            act()
        else:
            pl.when(cond)(act)

    def halo_start(copies, pad, k):
        for copy, can_send, _ in copies[:2]:
            guarded(can_send, copy.start)
        for copy, can_send, _ in copies[4:]:
            guarded(can_send, copy.start)
        strip_w[...] = pad[2 : rows + 2, 0:SIDE].reshape(rows * SIDE, channels).astype(F32)
        strip_e[...] = (
            pad[2 : rows + 2, cols - SIDE : cols].reshape(rows * SIDE, channels).astype(F32)
        )
        for j in range(2):
            strip_out[k, 0, j] = strip_w[pl.ds(j, rows, stride=SIDE)].astype(BF16)
            strip_out[k, 1, j] = strip_e[pl.ds(SIDE - 2 + j, rows, stride=SIDE)].astype(BF16)
        for copy, can_send, _ in copies[2:4]:
            guarded(can_send, copy.start)

    def halo_finish(copies, pad, k):
        for copy, _, can_recv in copies:
            guarded(can_recv, copy.wait_recv)
        for j in range(2):
            strip_z[pl.ds(j, rows, stride=SIDE)] = strip_in[k, 0, j].astype(F32)
            strip_z[pl.ds(SIDE - 2 + j, rows, stride=SIDE)] = strip_in[k, 1, j].astype(F32)
        pad[2 : rows + 2, side] = strip_z[...].astype(BF16).reshape(rows, SIDE, channels)
        at = lax.broadcasted_iota(jnp.int32, (4, SIDE, channels), 1)
        corner = jnp.where(
            at < 2, right[k].astype(F32), jnp.where(at >= SIDE - 2, left[k].astype(F32), 0.0)
        ).astype(BF16)
        pad[0:2, side] = corner[0:2]
        pad[rows + 2 : rows + 4, side] = corner[2:4]

    def halo_drain(copies):
        for copy, can_send, _ in copies:
            guarded(can_send, copy.wait_send)

    def place_weights(layer, turn):
        at = 2 * layer + turn
        for p in range(TAPS):
            for q in range(TAPS):
                if turn:
                    block = conv_ref[layer, TAPS - 1 - p, TAPS - 1 - q].T
                else:
                    block = conv_ref[layer, p, q]
                wbuf[at, p * channels : (p + 1) * channels, q * channels : (q + 1) * channels] = block

    group = 4 if rows % 4 == 0 else 1

    def conv(pad, at, finish, between=None):
        def one(b):
            lhs = jnp.concatenate(
                [pad[pl.ds(b * group + p, group)].reshape(group * wide, channels) for p in range(TAPS)],
                axis=1,
            )
            prod = jnp.dot(lhs, wbuf[at], preferred_element_type=F32)
            for r in range(group):
                total = None
                for q in range(TAPS):
                    piece = prod[r * wide : (r + 1) * wide, q * channels : (q + 1) * channels]
                    shift = (2 - q) % wide
                    if shift:
                        piece = pltpu.roll(piece, shift, 0)
                    piece = piece[:cols]
                    total = piece if total is None else total + piece
                finish(b * group + r, total)

        if between is None:
            pl.loop(0, rows // group)(one)
        else:
            for b in range(rows // group):
                one(b)
                between()

    def shift_grad(pad, at):
        @pl.loop(0, rows // group)
        def _(b):
            for r in range(group):
                h = b * group + r
                ext = jnp.concatenate(
                    [pad[h + 2, 0:cols].astype(F32), jnp.zeros((SIDE, channels), F32)], axis=0
                )
                for q in range(TAPS):
                    shift = (q - 2) % wide
                    moved = (pltpu.roll(ext, shift, 0) if shift else ext).astype(BF16)
                    lanes = slice(q * channels, (q + 1) * channels)
                    shifted[at, h, :, lanes] = moved[:cols]
                    shifted_side[at, h, :, lanes] = moved[cols:]

    def turn_act(pad):
        @pl.loop(0, rows // group)
        def _(b):
            for r in range(group):
                h = b * group + r + 2
                turned[h] = pad[h, 0:cols].T

    def turn_halo(pad):
        for h in (0, 1, rows + 2, rows + 3):
            turned[h] = pad[h, 0:cols].T

    def kernel_terms(pad, slot_of, between=None):
        side_lhs = jnp.concatenate(
            [pad[p : p + rows, side].reshape(rows * SIDE, channels).T for p in range(TAPS)], axis=0
        )
        kacc[...] = jnp.dot(
            side_lhs, shifted_side[slot_of].reshape(rows * SIDE, TAPS * channels),
            preferred_element_type=F32,
        )

        def one(b):
            lhs = jnp.concatenate(
                [
                    jnp.concatenate([turned[b * group + p + r] for r in range(group)], axis=1)
                    for p in range(TAPS)
                ],
                axis=0,
            )
            rhs = shifted[slot_of, pl.ds(b * group, group)].reshape(group * cols, TAPS * channels)
            kacc[...] += jnp.dot(lhs, rhs, preferred_element_type=F32)

        if between is None:
            pl.loop(0, rows // group)(one)
        else:
            for b in range(rows // group):
                one(b)
                between()
        per = channels // 16
        for p in range(TAPS):
            for q in range(TAPS):
                block = kacc[p * channels : (p + 1) * channels, q * channels : (q + 1) * channels]
                n = (p * TAPS + q) * per
                part[slot_of, n : n + per] = block.astype(BF16).reshape(per, 16, channels)
        used_tiles = TAPS * TAPS * per
        if used_tiles < tile_count:
            part[slot_of, used_tiles:] = jnp.zeros(
                (tile_count - used_tiles, 16, channels), BF16
            )

    leaving = []

    def sum_steps(slot_of, start, length, stream, plan):
        groups = [Group(stage, lat, lon) for stage in plan]
        pending = []
        base = start
        box = start
        whole = slice(start, start + length)
        nsem = 0
        bases = []
        for g in groups:
            share = length // g.size
            sent = []
            for dist in range(1, g.size):
                copy = pltpu.make_async_remote_copy(
                    src_ref=part.at[slot_of, pl.ds(base + g.rank_at(dist) * share, share)],
                    dst_ref=inbox.at[slot_of, pl.ds(box + (dist - 1) * share, share)],
                    send_sem=rs_send.at[stream, nsem], recv_sem=rs_recv.at[stream, nsem],
                    device_id=g.device(g.rank_at(dist)), device_id_type=MESH,
                )
                copy.start()
                sent.append(copy)
                nsem += 1
            pending += sent
            yield
            for copy in sent:
                copy.wait_recv()
            mine = base + g.rank * share
            total = part[slot_of, pl.ds(mine, share)].astype(F32)
            for dist in range(1, g.size):
                at = box + (dist - 1) * share
                total = total + inbox[slot_of, at : at + share].astype(F32)
            part[slot_of, pl.ds(mine, share)] = total.astype(BF16)
            box += (g.size - 1) * share
            bases.append(base)
            base, length = mine, share
        final[slot_of, pl.ds(base, length)] = part[slot_of, pl.ds(base, length)]
        nsem = 0
        for g, low in zip(reversed(groups), reversed(bases)):
            sent, got = [], []
            for dist in range(1, g.size):
                copy = pltpu.make_async_remote_copy(
                    src_ref=final.at[slot_of, pl.ds(base, length)],
                    dst_ref=final.at[slot_of, pl.ds(base, length)],
                    send_sem=ag_send.at[stream, nsem], recv_sem=ag_recv.at[stream, nsem],
                    device_id=g.device(g.rank_at(dist)), device_id_type=MESH,
                )
                copy.start()
                sent.append(copy)
                here = final.at[slot_of, pl.ds(low + g.rank_at(g.size - dist) * length, length)]
                got.append(
                    pltpu.make_async_remote_copy(
                        src_ref=here, dst_ref=here,
                        send_sem=ag_send.at[stream, nsem], recv_sem=ag_recv.at[stream, nsem],
                        device_id=g.device(g.rank_at(dist)), device_id_type=MESH,
                    )
                )
                nsem += 1
            pending += sent
            yield
            for copy in got:
                copy.wait_recv()
            base, length = low, length * g.size
        for copy in pending:
            copy.wait_send()
        copy = pltpu.make_async_copy(
            final.at[slot_of, whole], kgrad_ref.at[slot_of, whole], out_sem.at[stream]
        )
        copy.start()
        leaving.append(copy)

    def small_steps(plan):
        nsem = 0
        pending = []
        for n, stage in enumerate(plan):
            g = Group(stage, lat, lon)
            sent = []
            for dist in range(1, g.size):
                copy = pltpu.make_async_remote_copy(
                    src_ref=small.at[n], dst_ref=small_in.at[nsem],
                    send_sem=sm_send.at[nsem], recv_sem=sm_recv.at[nsem],
                    device_id=g.device(g.rank_at(dist)), device_id_type=MESH,
                )
                copy.start()
                sent.append((copy, nsem, dist))
                nsem += 1
            pending += sent
            yield
            for copy, _, _ in sent:
                copy.wait_recv()
            total = jnp.zeros(small.shape[1:], F32)
            mine = small[n].astype(F32)
            for rank in range(g.size):
                term = mine
                for _, box, dist in sent:
                    term = jnp.where(g.rank_at(g.size - dist) == rank, small_in[box].astype(F32), term)
                total = total + term
            small[n + 1] = total.astype(BF16)
        for copy, _, _ in pending:
            copy.wait_send()
        small_ref[...] = small[len(plan)]

    pad_g2[2 : rows + 2, 0:cols] = cot_ref[...]
    for k, pad in enumerate((pad_g2, pad_a1, pad_a2, pad_g1)):
        clear_edges(pad, k)
    strip_z[...] = jnp.zeros_like(strip_z)
    place_weights(1, True)
    field_count = fields_ref.shape[0]
    width = values_ref.shape[3]
    featx[width:, :] = jnp.zeros((featx.shape[0] - width, featx.shape[1]), BF16)
    field_rows[...] = fields_ref[...].astype(F32).reshape(field_count * rows, cols)
    for h in range(rows):
        featx[width : width + field_count, h * cols : (h + 1) * cols] = field_rows[
            pl.ds(h, field_count, stride=rows)
        ].astype(BF16)
    wcat[...] = jnp.zeros_like(wcat)
    wcat[0:width] = obs_w_ref[...]
    wcat[width : width + field_count] = field_w_ref[...]

    pl.semaphore_wait(barrier, parts - 1)

    @pl.loop(1, parts)
    def _(dist):
        peer, dev = device_at(dist)
        pltpu.make_async_remote_copy(
            src_ref=outgoing.at[peer], dst_ref=arrived.at[me],
            send_sem=a2a_send.at[dist], recv_sem=a2a_recv.at[dist],
            device_id=dev, device_id_type=MESH,
        ).start()

    arrived[me] = outgoing[me]
    halo_g2 = halo_copies(pad_g2, 0)
    halo_start(halo_g2, pad_g2, 0)
    shift_grad(pad_g2, 1)
    place_weights(0, False)
    halo_finish(halo_g2, pad_g2, 0)

    def keep_back(h, total):
        back2[h] = total

    conv(pad_g2, 3, keep_back)

    @pl.loop(1, parts)
    def _(dist):
        sender = lax.rem(me + parts - dist, parts)
        pltpu.make_async_remote_copy(
            src_ref=arrived.at[sender], dst_ref=arrived.at[sender],
            send_sem=a2a_send.at[dist], recv_sem=a2a_recv.at[dist],
            device_id=device_at(dist)[1], device_id_type=MESH,
        ).wait_recv()

    count = parts * capacity
    lane = lax.broadcasted_iota(jnp.int32, (count, 128), 1)
    pick = lane == lax.rem(lax.broadcasted_iota(jnp.int32, (count, 128), 0), capacity)

    head = arrived[:, capacity:].astype(F32)

    def column(n):
        spread = jnp.broadcast_to(head[:, n : n + 1, :], (parts, capacity, 128)).reshape(count, 128)
        return jnp.sum(jnp.where(pick, spread, 0.0), axis=1, keepdims=True)

    w_col, cell_col = column(0), column(1) * cols + column(2)
    values_t = jnp.concatenate(
        [arrived[:, 0:capacity].reshape(count, width).T, jnp.ones((16, count), BF16)], axis=0
    )
    block = 512 if (rows * cols) % 512 == 0 else cols

    @pl.loop(0, rows * cols // block)
    def _(b):
        start = pl.multiple_of(b * block, block)
        ids = (start + lax.broadcasted_iota(jnp.int32, (count, block), 1)).astype(F32)
        spread = jnp.where(ids == cell_col, w_col, 0.0).astype(BF16)
        sums = jnp.dot(values_t, spread, preferred_element_type=F32)
        dens = sums[width : width + 1]
        featx[0:width, pl.ds(start, block)] = (sums[0:width] / (1.0 + dens)).astype(BF16)

    @pl.loop(0, rows // group)
    def _(b):
        start = pl.multiple_of(b * group * cols, group * cols)
        feats = featx[:, pl.ds(start, group * cols)].T
        x = jnp.dot(feats, wcat[...], preferred_element_type=F32).astype(BF16).astype(F32)
        x = x.reshape(group, cols, channels)
        act, slope = gelu_pair(x)
        at = pl.ds(b * group, group)
        x_keep[at] = x
        slope1[at] = slope
        pad_a1[pl.ds(b * group + 2, group), 0:cols] = act.astype(BF16)

    halo_a1 = halo_copies(pad_a1, 1)
    halo_start(halo_a1, pad_a1, 1)
    turn_act(pad_a1)
    halo_finish(halo_a1, pad_a1, 1)
    turn_halo(pad_a1)

    def first_layer(h, total):
        x = (x_keep[h] + total).astype(BF16).astype(F32)
        act, slope = gelu_pair(x)
        x_keep[h] = x
        pad_a2[h + 2, 0:cols] = act.astype(BF16)
        g = cot_ref[h].astype(F32) + slope * back2[h]
        pad_g1[h + 2, 0:cols] = g.astype(BF16)

    conv(pad_a1, 0, first_layer, lambda: None)
    halo_a2 = halo_copies(pad_a2, 2)
    halo_start(halo_a2, pad_a2, 2)
    halo_g1 = halo_copies(pad_g1, 3)
    halo_start(halo_g1, pad_g1, 3)

    lat_plan = stage_plan(lat_parts, lon_parts, True)
    lon_plan = stage_plan(lat_parts, lon_parts, False)
    first_part = tile_count // (2 * parts) * parts
    live = []

    def start_sums(slot_of):
        spans = [(0, first_part), (first_part, tile_count - first_part)]
        for n, (start, length) in enumerate(spans):
            if length:
                steps = sum_steps(slot_of, start, length, 2 * slot_of + n, lon_plan if n == 0 else lat_plan)
                next(steps)
                live.append(steps)

    def tick(count=1):
        for _ in range(count):
            if live:
                steps = live.pop(0)
                if next(steps, "end") != "end":
                    live.append(steps)

    shift_grad(pad_g1, 0)
    kernel_terms(pad_a1, 0)
    start_sums(0)

    turn_act(pad_a2)
    halo_finish(halo_a2, pad_a2, 2)
    turn_halo(pad_a2)
    tick(2)
    kernel_terms(pad_a2, 1, tick)
    start_sums(1)
    place_weights(0, True)
    halo_finish(halo_g1, pad_g1, 3)
    tick(2)

    def last_grad(h, total):
        g = pad_g1[h + 2, 0:cols].astype(F32) + slope1[h] * total
        back2[h] = g

    conv(pad_g1, 1, last_grad, lambda: tick(2))
    grads = jnp.dot(
        featx[...], back2[...].astype(BF16).reshape(rows * cols, channels), preferred_element_type=F32
    )
    small[0] = grads[0 : small.shape[1]].astype(BF16)
    sum_c = small_steps(lat_plan)
    next(sum_c)
    live.insert(0, sum_c)

    place_weights(1, False)

    def last_layer(h, total):
        enc_keep[h] = (x_keep[h] + total).astype(BF16)

    conv(pad_a2, 2, last_layer, lambda: tick(3))
    copy = pltpu.make_async_copy(enc_keep, enc_ref, out_sem.at[4])
    copy.start()
    leaving.append(copy)
    while live:
        tick()

    for copies in (halo_g2, halo_a1, halo_a2, halo_g1):
        halo_drain(copies)

    @pl.loop(1, parts)
    def _(dist):
        peer, dev = device_at(dist)
        pltpu.make_async_remote_copy(
            src_ref=outgoing.at[peer], dst_ref=arrived.at[me],
            send_sem=a2a_send.at[dist], recv_sem=a2a_recv.at[dist],
            device_id=dev, device_id_type=MESH,
        ).wait_send()

    for copy in leaving:
        copy.wait()


def widen(
    scale, chunks, enc_in, kgrad_in, small_in, enc_out, kgrad_out, obs_out, field_out,
    narrow, stage, enc_keep, in_sems, out_sems,
):
    per = stage.shape[1] // chunks
    spans = [(n // chunks, slice(n % chunks * per, (n % chunks + 1) * per)) for n in range(2 * chunks)]
    loads = [
        pltpu.make_async_copy(kgrad_in.at[at], narrow.at[at], in_sems.at[n])
        for n, at in enumerate(spans)
    ]
    loads.append(pltpu.make_async_copy(enc_in, enc_keep, in_sems.at[2 * chunks]))
    for copy in loads:
        copy.start()
    stores = []
    for n, at in enumerate(spans):
        loads[n].wait()
        stage[at] = scale * narrow[at].astype(F32)
        stores.append(pltpu.make_async_copy(stage.at[at], kgrad_out.at[at], out_sems.at[n]))
        stores[-1].start()
    loads[-1].wait()
    stores.append(pltpu.make_async_copy(enc_keep, enc_out, out_sems.at[2 * chunks]))
    stores[-1].start()
    wide = scale * small_in[...].astype(F32)
    obs_out[...] = wide[: obs_out.shape[0]]
    field_out[...] = wide[obs_out.shape[0] : obs_out.shape[0] + field_out.shape[0]]
    for copy in stores:
        copy.wait()


def per_device(
    grid_fields, obs_values, obs_count, obs_cell, obs_valid, obs_dist2,
    field_weight, obs_weight, conv_kernel, cotangent,
):
    rows, cols, channels = cotangent.shape
    lat_parts = lax.axis_size("lat")
    lon_parts = lax.axis_size("lon")
    parts = lat_parts * lon_parts
    fields = grid_fields.shape[0]
    width = obs_values.shape[3]
    capacity = obs_values.shape[2]
    wide = cols + SIDE
    tiles = TAPS * TAPS * channels // 16
    tiles = -(-tiles // parts) * parts
    plan = stage_plan(lat_parts, lon_parts, True)
    hops = sum(stage[1] - 1 for stage in plan)
    deep = -(-(width + fields) // 128) * 128
    small_rows = -(-(width + fields) // 16) * 16
    vmem = pl.BlockSpec(memory_space=pltpu.VMEM)
    anywhere = pl.BlockSpec(memory_space=pl.ANY)
    pads = [pltpu.VMEM((rows + 4, wide, channels), BF16)] * 4
    encoded, kgrad, small = pl.pallas_call(
        functools.partial(kernel, lat_parts, lon_parts),
        out_shape=(
            jax.ShapeDtypeStruct((rows, cols, channels), BF16),
            jax.ShapeDtypeStruct((2, tiles, 16, channels), BF16),
            jax.ShapeDtypeStruct((small_rows, channels), BF16),
        ),
        in_specs=[vmem] * 10,
        out_specs=(anywhere, anywhere, vmem),
        scratch_shapes=[
            pltpu.VMEM((parts, 3, 128), F32),
            pltpu.VMEM((parts, capacity + 16, width), BF16),
            pltpu.VMEM((parts, capacity + 16, width), BF16),
            pltpu.VMEM((rows, cols, channels), BF16),
            pltpu.VMEM((deep, rows * cols), BF16),
            pltpu.VMEM((deep, channels), BF16),
            pltpu.VMEM((4, TAPS * channels, TAPS * channels), BF16),
            *pads,
            pltpu.VMEM((4, 4, SIDE, channels), BF16),
            pltpu.VMEM((4, 4, SIDE, channels), BF16),
            pltpu.VMEM((4, 2, 2, rows, channels), BF16),
            pltpu.VMEM((4, 2, 2, rows, channels), BF16),
            pltpu.VMEM((rows * SIDE, channels), F32),
            pltpu.VMEM((rows * SIDE, channels), F32),
            pltpu.VMEM((rows * SIDE, channels), F32),
            pltpu.VMEM((fields * rows, cols), F32),
            pltpu.VMEM((rows + 4, channels, cols), BF16),
            pltpu.VMEM((2, rows, cols, TAPS * channels), BF16),
            pltpu.VMEM((2, rows, SIDE, TAPS * channels), BF16),
            pltpu.VMEM((rows, cols, channels), F32),
            pltpu.VMEM((rows, cols, channels), F32),
            pltpu.VMEM((rows, cols, channels), F32),
            pltpu.VMEM((TAPS * channels, TAPS * channels), F32),
            pltpu.VMEM((2, tiles, 16, channels), BF16),
            pltpu.VMEM((2, tiles, 16, channels), BF16),
            pltpu.VMEM((2, tiles, 16, channels), BF16),
            pltpu.VMEM((len(plan) + 1, small_rows, channels), BF16),
            pltpu.VMEM((hops, small_rows, channels), BF16),
            pltpu.SemaphoreType.DMA((parts,)),
            pltpu.SemaphoreType.DMA((parts,)),
            pltpu.SemaphoreType.DMA((5,)),
            pltpu.SemaphoreType.DMA((4, 8)),
            pltpu.SemaphoreType.DMA((4, 8)),
            pltpu.SemaphoreType.DMA((4, hops)),
            pltpu.SemaphoreType.DMA((4, hops)),
            pltpu.SemaphoreType.DMA((4, hops)),
            pltpu.SemaphoreType.DMA((4, hops)),
            pltpu.SemaphoreType.DMA((hops,)),
            pltpu.SemaphoreType.DMA((hops,)),
        ],
        compiler_params=pltpu.CompilerParams(
            collective_id=0, has_side_effects=True, vmem_limit_bytes=56 * 1024 * 1024
        ),
        name="encoder",
    )(
        grid_fields, obs_values, obs_count, jnp.swapaxes(obs_cell, 1, 2),
        jnp.swapaxes(obs_valid, 1, 2), jnp.swapaxes(obs_dist2, 1, 2),
        field_weight, obs_weight, conv_kernel, cotangent,
    )
    scale = 1.0 / (rows * lat_parts * cols * lon_parts) ** 0.5
    used = TAPS * TAPS * channels // 16
    chunks = math.gcd(used, 4)
    encoded, kernel_grad, obs_grad, field_grad = pl.pallas_call(
        functools.partial(widen, scale, chunks),
        in_specs=[anywhere] * 2 + [vmem],
        out_specs=[anywhere] * 2 + [vmem] * 2,
        out_shape=(
            jax.ShapeDtypeStruct((rows, cols, channels), BF16),
            jax.ShapeDtypeStruct((2, used, 16, channels), F32),
            jax.ShapeDtypeStruct((width, channels), F32),
            jax.ShapeDtypeStruct((fields, channels), F32),
        ),
        scratch_shapes=[
            pltpu.VMEM((2, used, 16, channels), BF16),
            pltpu.VMEM((2, used, 16, channels), F32),
            pltpu.VMEM((rows, cols, channels), BF16),
            pltpu.SemaphoreType.DMA((2 * chunks + 1,)),
            pltpu.SemaphoreType.DMA((2 * chunks + 1,)),
        ],
        compiler_params=pltpu.CompilerParams(vmem_limit_bytes=56 * 1024 * 1024),
        name="widen",
    )(encoded, kgrad, small)
    return encoded, kernel_grad.reshape(2, TAPS, TAPS, channels, channels), obs_grad, field_grad


def solution(mesh):
    return jax.shard_map(
        per_device,
        mesh=mesh,
        in_specs=(
            P(None, "lat", "lon"),
            P(("lat", "lon"), None, None, None),
            P(("lat", "lon"), None),
            P(("lat", "lon"), None, None),
            P(("lat", "lon"), None, None),
            P(("lat", "lon"), None, None),
            P(),
            P(),
            P(),
            P("lat", "lon", None),
        ),
        out_specs=(P("lat", "lon", None), P(), P(), P()),
        check_vma=False,
    )
```

```python
import functools
import math

import jax
import jax.numpy as jnp
from jax import lax
from jax.experimental import pallas as pl
from jax.experimental.pallas import tpu as pltpu
from jax.sharding import PartitionSpec as P

BF16 = jnp.bfloat16
F32 = jnp.float32
MESH = pl.DeviceIdType.MESH
TAPS = 5
SIDE = 16
ROOT = 0.7978845608028654


def gelu_pair(x):
    cubic = 0.044715 * x * x
    bend = jnp.tanh(ROOT * x * (1.0 + cubic))
    half = 0.5 * (1.0 + bend)
    slope = half + 0.5 * x * (1.0 - bend * bend) * (ROOT * (1.0 + 3.0 * cubic))
    return x * half, slope


def stage_plan(lat_parts, lon_parts, lat_first):
    lat = [("lat", 2, 1), ("lat", lat_parts // 2, 2)] if lat_parts % 2 == 0 else [("lat", lat_parts, 1)]
    lon = [("lon", 2, 1), ("lon", lon_parts // 2, 2)] if lon_parts % 2 == 0 else [("lon", lon_parts, 1)]
    if lat_first:
        plan = lat + lon
    else:
        plan = lat[:1] + lon[:1] + lat[1:] + lon[1:]
    return [stage for stage in plan if stage[1] > 1]


class Group:
    def __init__(self, stage, lat, lon):
        self.axis, self.size, self.stride = stage
        self.lat, self.lon = lat, lon
        pos = lat if self.axis == "lat" else lon
        self.rank = lax.rem(pos // self.stride, self.size)
        self.pos = pos

    def rank_at(self, dist):
        return lax.rem(self.rank + dist, self.size)

    def device(self, rank):
        pos = self.pos + (rank - self.rank) * self.stride
        return (pos, self.lon) if self.axis == "lat" else (self.lat, pos)


def kernel(
    lat_parts, lon_parts,
    fields_ref, values_hbm, count_ref, cell_ref, valid_ref, dist_ref,
    field_w_ref, obs_w_ref, conv_hbm, cot_hbm,
    enc_ref, kgrad_ref, small_ref,
    conv_ref, cot_ref, header, outgoing, arrived, enc_keep, featx, wcat, wbuf, pad_g2, pad_a1, pad_a2, pad_g1,
    left, right, strip_out, strip_in, strip_w, strip_e, strip_z, field_rows,
    turned, shifted, shifted_side, back2, x_keep, slope1,
    kacc, part, final, inbox, small, small_in,
    a2a_send, a2a_recv, in_sem, out_sem, halo_send, halo_recv,
    rs_send, rs_recv, ag_send, ag_recv, sm_send, sm_recv,
):
    lat = lax.axis_index("lat")
    lon = lax.axis_index("lon")
    parts = lat_parts * lon_parts
    me = lat * lon_parts + lon
    rows, cols, channels = cot_ref.shape
    capacity, width = values_hbm.shape[2:]
    side = slice(cols, cols + SIDE)
    wide = cols + SIDE
    tile_count = part.shape[1]

    def device_at(dist):
        peer = lax.rem(me + dist, parts)
        return peer, (lax.div(peer, lon_parts), lax.rem(peer, lon_parts))

    barrier = pltpu.get_barrier_semaphore()

    @pl.loop(1, parts)
    def _(dist):
        pl.semaphore_signal(barrier, inc=1, device_id=device_at(dist)[1], device_id_type=MESH)

    load_rows = pltpu.make_async_copy(
        values_hbm.at[0], outgoing.at[:, pl.ds(0, capacity)], in_sem.at[0]
    )
    load_cot = pltpu.make_async_copy(cot_hbm, cot_ref, in_sem.at[1])
    load_conv = [
        pltpu.make_async_copy(conv_hbm.at[n], conv_ref.at[n], in_sem.at[2 + n]) for n in range(2)
    ]
    for copy in (load_rows, load_cot, load_conv[1], load_conv[0]):
        copy.start()

    slot = lax.broadcasted_iota(jnp.int32, (capacity, parts), 0)
    used = (valid_ref[0] == 1) & (slot < count_ref[...])
    weight = jnp.where(used, jnp.exp(-0.5 * dist_ref[0]), 0.0).astype(BF16).astype(F32)
    header[...] = jnp.zeros_like(header)
    header[:, 0, 0:capacity] = weight.T
    cells = cell_ref[0].astype(F32)
    cell_row = jnp.floor(cells / cols)
    header[:, 1, 0:capacity] = cell_row.T
    header[:, 2, 0:capacity] = (cells - cell_row * cols).T
    line = lax.broadcasted_iota(jnp.int32, (parts, 16, 128), 1)
    head = jnp.zeros((parts, 16, 128), F32)
    for n in range(3):
        head = jnp.where(line == n, jnp.broadcast_to(header[:, n : n + 1, :], head.shape), head)
    outgoing[:, capacity:] = head.astype(BF16)

    def clear_edges(pad, k):
        zero = jnp.zeros((2, wide, channels), BF16)
        zero_side = jnp.zeros((2, SIDE, channels), BF16)

        @pl.when(lat == 0)
        def _():
            pad[0:2] = zero
            left[k, 0:2] = zero_side
            right[k, 0:2] = zero_side

        @pl.when(lat == lat_parts - 1)
        def _():
            pad[rows + 2 : rows + 4] = zero
            left[k, 2:4] = zero_side
            right[k, 2:4] = zero_side

    def halo_copies(pad, k):
        up, down = lat - 1, lat + 1
        west = lax.rem(lon + lon_parts - 1, lon_parts)
        east = lax.rem(lon + 1, lon_parts)
        first, last = slice(2, 4), slice(rows, rows + 2)
        above, below = slice(0, 2), slice(rows + 2, rows + 4)
        top, bottom = slice(0, 2), slice(2, 4)
        lo, hi, full = slice(0, SIDE), slice(cols - SIDE, cols), slice(0, cols)
        has_up, has_down = lat > 0, lat < lat_parts - 1
        table = [
            (pad.at[first, full], pad.at[below, full], (up, lon), has_up, has_down),
            (pad.at[last, full], pad.at[above, full], (down, lon), has_down, has_up),
            (strip_out.at[k, 0], strip_in.at[k, 0], (lat, west), None, None),
            (strip_out.at[k, 1], strip_in.at[k, 1], (lat, east), None, None),
            (pad.at[first, lo], right.at[k, bottom], (up, west), has_up, has_down),
            (pad.at[first, hi], left.at[k, bottom], (up, east), has_up, has_down),
            (pad.at[last, lo], right.at[k, top], (down, west), has_down, has_up),
            (pad.at[last, hi], left.at[k, top], (down, east), has_down, has_up),
        ]
        out = []
        for n, (src, dst, dev, can_send, can_recv) in enumerate(table):
            copy = pltpu.make_async_remote_copy(
                src_ref=src, dst_ref=dst, send_sem=halo_send.at[k, n], recv_sem=halo_recv.at[k, n],
                device_id=dev, device_id_type=MESH,
            )
            out.append((copy, can_send, can_recv))
        return out

    def guarded(cond, act):
        if cond is None:
            act()
        else:
            pl.when(cond)(act)

    def halo_start(copies, pad, k):
        for copy, can_send, _ in copies[:2]:
            guarded(can_send, copy.start)
        for copy, can_send, _ in copies[4:]:
            guarded(can_send, copy.start)
        strip_w[...] = pad[2 : rows + 2, 0:SIDE].reshape(rows * SIDE, channels).astype(F32)
        strip_e[...] = (
            pad[2 : rows + 2, cols - SIDE : cols].reshape(rows * SIDE, channels).astype(F32)
        )
        for j in range(2):
            strip_out[k, 0, j] = strip_w[pl.ds(j, rows, stride=SIDE)].astype(BF16)
            strip_out[k, 1, j] = strip_e[pl.ds(SIDE - 2 + j, rows, stride=SIDE)].astype(BF16)
        for copy, can_send, _ in copies[2:4]:
            guarded(can_send, copy.start)

    def halo_finish(copies, pad, k):
        for copy, _, can_recv in copies:
            guarded(can_recv, copy.wait_recv)
        for j in range(2):
            strip_z[pl.ds(j, rows, stride=SIDE)] = strip_in[k, 0, j].astype(F32)
            strip_z[pl.ds(SIDE - 2 + j, rows, stride=SIDE)] = strip_in[k, 1, j].astype(F32)
        pad[2 : rows + 2, side] = strip_z[...].astype(BF16).reshape(rows, SIDE, channels)
        at = lax.broadcasted_iota(jnp.int32, (4, SIDE, channels), 1)
        corner = jnp.where(
            at < 2, right[k].astype(F32), jnp.where(at >= SIDE - 2, left[k].astype(F32), 0.0)
        ).astype(BF16)
        pad[0:2, side] = corner[0:2]
        pad[rows + 2 : rows + 4, side] = corner[2:4]

    def halo_drain(copies):
        for copy, can_send, _ in copies:
            guarded(can_send, copy.wait_send)

    def place_weights(layer, turn):
        at = 2 * layer + turn
        for p in range(TAPS):
            for q in range(TAPS):
                if turn:
                    block = conv_ref[layer, TAPS - 1 - p, TAPS - 1 - q].T
                else:
                    block = conv_ref[layer, p, q]
                wbuf[at, p * channels : (p + 1) * channels, q * channels : (q + 1) * channels] = block

    group = 4 if rows % 4 == 0 else 1

    def conv(pad, at, finish, between=None):
        def one(b):
            lhs = jnp.concatenate(
                [pad[pl.ds(b * group + p, group)].reshape(group * wide, channels) for p in range(TAPS)],
                axis=1,
            )
            prod = jnp.dot(lhs, wbuf[at], preferred_element_type=F32)
            for r in range(group):
                total = None
                for q in range(TAPS):
                    piece = prod[r * wide : (r + 1) * wide, q * channels : (q + 1) * channels]
                    shift = (2 - q) % wide
                    if shift:
                        piece = pltpu.roll(piece, shift, 0)
                    piece = piece[:cols]
                    total = piece if total is None else total + piece
                finish(b * group + r, total)

        if between is None:
            pl.loop(0, rows // group)(one)
        else:
            for b in range(rows // group):
                one(b)
                between()

    def shift_grad(pad, at):
        @pl.loop(0, rows // group)
        def _(b):
            for r in range(group):
                h = b * group + r
                ext = jnp.concatenate(
                    [pad[h + 2, 0:cols].astype(F32), jnp.zeros((SIDE, channels), F32)], axis=0
                )
                for q in range(TAPS):
                    shift = (q - 2) % wide
                    moved = (pltpu.roll(ext, shift, 0) if shift else ext).astype(BF16)
                    lanes = slice(q * channels, (q + 1) * channels)
                    shifted[at, h, :, lanes] = moved[:cols]
                    shifted_side[at, h, :, lanes] = moved[cols:]

    def turn_act(pad):
        @pl.loop(0, rows // group)
        def _(b):
            for r in range(group):
                h = b * group + r + 2
                turned[h] = pad[h, 0:cols].T

    def turn_halo(pad):
        for h in (0, 1, rows + 2, rows + 3):
            turned[h] = pad[h, 0:cols].T

    def kernel_terms(pad, slot_of, between=None):
        side_lhs = jnp.concatenate(
            [pad[p : p + rows, side].reshape(rows * SIDE, channels).T for p in range(TAPS)], axis=0
        )
        kacc[...] = jnp.dot(
            side_lhs, shifted_side[slot_of].reshape(rows * SIDE, TAPS * channels),
            preferred_element_type=F32,
        )

        def one(b):
            lhs = jnp.concatenate(
                [
                    jnp.concatenate([turned[b * group + p + r] for r in range(group)], axis=1)
                    for p in range(TAPS)
                ],
                axis=0,
            )
            rhs = shifted[slot_of, pl.ds(b * group, group)].reshape(group * cols, TAPS * channels)
            kacc[...] += jnp.dot(lhs, rhs, preferred_element_type=F32)

        if between is None:
            pl.loop(0, rows // group)(one)
        else:
            for b in range(rows // group):
                one(b)
                between()
        per = channels // 16
        for p in range(TAPS):
            for q in range(TAPS):
                block = kacc[p * channels : (p + 1) * channels, q * channels : (q + 1) * channels]
                n = (p * TAPS + q) * per
                part[slot_of, n : n + per] = block.astype(BF16).reshape(per, 16, channels)
        used_tiles = TAPS * TAPS * per
        if used_tiles < tile_count:
            part[slot_of, used_tiles:] = jnp.zeros(
                (tile_count - used_tiles, 16, channels), BF16
            )

    leaving = []

    def sum_steps(slot_of, start, length, stream, plan):
        groups = [Group(stage, lat, lon) for stage in plan]
        pending = []
        base = start
        box = start
        whole = slice(start, start + length)
        nsem = 0
        bases = []
        for g in groups:
            share = length // g.size
            sent = []
            for dist in range(1, g.size):
                copy = pltpu.make_async_remote_copy(
                    src_ref=part.at[slot_of, pl.ds(base + g.rank_at(dist) * share, share)],
                    dst_ref=inbox.at[slot_of, pl.ds(box + (dist - 1) * share, share)],
                    send_sem=rs_send.at[stream, nsem], recv_sem=rs_recv.at[stream, nsem],
                    device_id=g.device(g.rank_at(dist)), device_id_type=MESH,
                )
                copy.start()
                sent.append(copy)
                nsem += 1
            pending += sent
            yield
            for copy in sent:
                copy.wait_recv()
            mine = base + g.rank * share
            total = part[slot_of, pl.ds(mine, share)].astype(F32)
            for dist in range(1, g.size):
                at = box + (dist - 1) * share
                total = total + inbox[slot_of, at : at + share].astype(F32)
            part[slot_of, pl.ds(mine, share)] = total.astype(BF16)
            box += (g.size - 1) * share
            bases.append(base)
            base, length = mine, share
        final[slot_of, pl.ds(base, length)] = part[slot_of, pl.ds(base, length)]
        nsem = 0
        for g, low in zip(reversed(groups), reversed(bases)):
            sent, got = [], []
            for dist in range(1, g.size):
                copy = pltpu.make_async_remote_copy(
                    src_ref=final.at[slot_of, pl.ds(base, length)],
                    dst_ref=final.at[slot_of, pl.ds(base, length)],
                    send_sem=ag_send.at[stream, nsem], recv_sem=ag_recv.at[stream, nsem],
                    device_id=g.device(g.rank_at(dist)), device_id_type=MESH,
                )
                copy.start()
                sent.append(copy)
                here = final.at[slot_of, pl.ds(low + g.rank_at(g.size - dist) * length, length)]
                got.append(
                    pltpu.make_async_remote_copy(
                        src_ref=here, dst_ref=here,
                        send_sem=ag_send.at[stream, nsem], recv_sem=ag_recv.at[stream, nsem],
                        device_id=g.device(g.rank_at(dist)), device_id_type=MESH,
                    )
                )
                nsem += 1
            pending += sent
            yield
            for copy in got:
                copy.wait_recv()
            base, length = low, length * g.size
        for copy in pending:
            copy.wait_send()
        copy = pltpu.make_async_copy(
            final.at[slot_of, whole], kgrad_ref.at[slot_of, whole], out_sem.at[stream]
        )
        copy.start()
        leaving.append(copy)

    def small_steps(plan):
        nsem = 0
        pending = []
        for n, stage in enumerate(plan):
            g = Group(stage, lat, lon)
            sent = []
            for dist in range(1, g.size):
                copy = pltpu.make_async_remote_copy(
                    src_ref=small.at[n], dst_ref=small_in.at[nsem],
                    send_sem=sm_send.at[nsem], recv_sem=sm_recv.at[nsem],
                    device_id=g.device(g.rank_at(dist)), device_id_type=MESH,
                )
                copy.start()
                sent.append((copy, nsem, dist))
                nsem += 1
            pending += sent
            yield
            for copy, _, _ in sent:
                copy.wait_recv()
            total = jnp.zeros(small.shape[1:], F32)
            mine = small[n].astype(F32)
            for rank in range(g.size):
                term = mine
                for _, box, dist in sent:
                    term = jnp.where(g.rank_at(g.size - dist) == rank, small_in[box].astype(F32), term)
                total = total + term
            small[n + 1] = total.astype(BF16)
        for copy, _, _ in pending:
            copy.wait_send()
        small_ref[...] = small[len(plan)]

    load_cot.wait()
    pad_g2[2 : rows + 2, 0:cols] = cot_ref[...]
    for k, pad in enumerate((pad_g2, pad_a1, pad_a2, pad_g1)):
        clear_edges(pad, k)
    strip_z[...] = jnp.zeros_like(strip_z)
    field_count = fields_ref.shape[0]
    featx[width:, :] = jnp.zeros((featx.shape[0] - width, featx.shape[1]), BF16)
    field_rows[...] = fields_ref[...].astype(F32).reshape(field_count * rows, cols)
    for h in range(rows):
        featx[width : width + field_count, h * cols : (h + 1) * cols] = field_rows[
            pl.ds(h, field_count, stride=rows)
        ].astype(BF16)
    wcat[...] = jnp.zeros_like(wcat)
    wcat[0:width] = obs_w_ref[...]
    wcat[width : width + field_count] = field_w_ref[...]

    load_conv[1].wait()
    place_weights(1, True)
    load_rows.wait()

    pl.semaphore_wait(barrier, parts - 1)

    @pl.loop(1, parts)
    def _(dist):
        peer, dev = device_at(dist)
        pltpu.make_async_remote_copy(
            src_ref=outgoing.at[peer], dst_ref=arrived.at[me],
            send_sem=a2a_send.at[dist], recv_sem=a2a_recv.at[dist],
            device_id=dev, device_id_type=MESH,
        ).start()

    arrived[me] = outgoing[me]
    halo_g2 = halo_copies(pad_g2, 0)
    halo_start(halo_g2, pad_g2, 0)
    shift_grad(pad_g2, 1)
    load_conv[0].wait()
    place_weights(0, False)
    halo_finish(halo_g2, pad_g2, 0)

    def keep_back(h, total):
        back2[h] = total

    conv(pad_g2, 3, keep_back)

    @pl.loop(1, parts)
    def _(dist):
        sender = lax.rem(me + parts - dist, parts)
        pltpu.make_async_remote_copy(
            src_ref=arrived.at[sender], dst_ref=arrived.at[sender],
            send_sem=a2a_send.at[dist], recv_sem=a2a_recv.at[dist],
            device_id=device_at(dist)[1], device_id_type=MESH,
        ).wait_recv()

    count = parts * capacity
    lane = lax.broadcasted_iota(jnp.int32, (count, 128), 1)
    pick = lane == lax.rem(lax.broadcasted_iota(jnp.int32, (count, 128), 0), capacity)

    head = arrived[:, capacity:].astype(F32)

    def column(n):
        spread = jnp.broadcast_to(head[:, n : n + 1, :], (parts, capacity, 128)).reshape(count, 128)
        return jnp.sum(jnp.where(pick, spread, 0.0), axis=1, keepdims=True)

    w_col, cell_col = column(0), column(1) * cols + column(2)
    values_t = jnp.concatenate(
        [arrived[:, 0:capacity].reshape(count, width).T, jnp.ones((16, count), BF16)], axis=0
    )
    block = 512 if (rows * cols) % 512 == 0 else cols

    @pl.loop(0, rows * cols // block)
    def _(b):
        start = pl.multiple_of(b * block, block)
        ids = (start + lax.broadcasted_iota(jnp.int32, (count, block), 1)).astype(F32)
        spread = jnp.where(ids == cell_col, w_col, 0.0).astype(BF16)
        sums = jnp.dot(values_t, spread, preferred_element_type=F32)
        dens = sums[width : width + 1]
        featx[0:width, pl.ds(start, block)] = (sums[0:width] / (1.0 + dens)).astype(BF16)

    @pl.loop(0, rows // group)
    def _(b):
        start = pl.multiple_of(b * group * cols, group * cols)
        feats = featx[:, pl.ds(start, group * cols)].T
        x = jnp.dot(feats, wcat[...], preferred_element_type=F32).astype(BF16).astype(F32)
        x = x.reshape(group, cols, channels)
        act, slope = gelu_pair(x)
        at = pl.ds(b * group, group)
        x_keep[at] = x
        slope1[at] = slope
        pad_a1[pl.ds(b * group + 2, group), 0:cols] = act.astype(BF16)

    halo_a1 = halo_copies(pad_a1, 1)
    halo_start(halo_a1, pad_a1, 1)
    turn_act(pad_a1)
    halo_finish(halo_a1, pad_a1, 1)
    turn_halo(pad_a1)

    def first_layer(h, total):
        x = (x_keep[h] + total).astype(BF16).astype(F32)
        act, slope = gelu_pair(x)
        x_keep[h] = x
        pad_a2[h + 2, 0:cols] = act.astype(BF16)
        g = cot_ref[h].astype(F32) + slope * back2[h]
        pad_g1[h + 2, 0:cols] = g.astype(BF16)

    conv(pad_a1, 0, first_layer)
    halo_a2 = halo_copies(pad_a2, 2)
    halo_start(halo_a2, pad_a2, 2)
    halo_g1 = halo_copies(pad_g1, 3)
    halo_start(halo_g1, pad_g1, 3)

    lat_plan = stage_plan(lat_parts, lon_parts, True)
    lon_plan = stage_plan(lat_parts, lon_parts, False)
    first_part = tile_count // (2 * parts) * parts
    live = []

    def start_sums(slot_of):
        spans = [(0, first_part), (first_part, tile_count - first_part)]
        for n, (start, length) in enumerate(spans):
            if length:
                steps = sum_steps(slot_of, start, length, 2 * slot_of + n, lon_plan if n == 0 else lat_plan)
                next(steps)
                live.append(steps)

    def tick(count=1):
        for _ in range(count):
            if live:
                steps = live.pop(0)
                if next(steps, "end") != "end":
                    live.append(steps)

    shift_grad(pad_g1, 0)
    kernel_terms(pad_a1, 0)
    start_sums(0)

    turn_act(pad_a2)
    halo_finish(halo_a2, pad_a2, 2)
    turn_halo(pad_a2)
    tick(2)
    kernel_terms(pad_a2, 1)
    start_sums(1)
    tick(2)
    place_weights(0, True)
    halo_finish(halo_g1, pad_g1, 3)
    tick(2)

    def last_grad(h, total):
        g = pad_g1[h + 2, 0:cols].astype(F32) + slope1[h] * total
        back2[h] = g

    conv(pad_g1, 1, last_grad, lambda: tick(2))
    grads = jnp.dot(
        featx[...], back2[...].astype(BF16).reshape(rows * cols, channels), preferred_element_type=F32
    )
    small[0] = grads[0 : small.shape[1]].astype(BF16)
    sum_c = small_steps(lat_plan)
    next(sum_c)
    live.insert(0, sum_c)

    place_weights(1, False)

    def last_layer(h, total):
        enc_keep[h] = (x_keep[h] + total).astype(BF16)

    conv(pad_a2, 2, last_layer, lambda: tick(3))
    copy = pltpu.make_async_copy(enc_keep, enc_ref, out_sem.at[4])
    copy.start()
    leaving.append(copy)
    while live:
        tick()

    for copies in (halo_g2, halo_a1, halo_a2, halo_g1):
        halo_drain(copies)

    @pl.loop(1, parts)
    def _(dist):
        peer, dev = device_at(dist)
        pltpu.make_async_remote_copy(
            src_ref=outgoing.at[peer], dst_ref=arrived.at[me],
            send_sem=a2a_send.at[dist], recv_sem=a2a_recv.at[dist],
            device_id=dev, device_id_type=MESH,
        ).wait_send()

    for copy in leaving:
        copy.wait()


def widen(
    scale, chunks, enc_in, kgrad_in, small_in, enc_out, kgrad_out, obs_out, field_out,
    narrow, stage, enc_keep, in_sems, out_sems,
):
    per = stage.shape[1] // chunks
    spans = [(n // chunks, slice(n % chunks * per, (n % chunks + 1) * per)) for n in range(2 * chunks)]
    loads = [
        pltpu.make_async_copy(kgrad_in.at[at], narrow.at[at], in_sems.at[n])
        for n, at in enumerate(spans)
    ]
    loads.append(pltpu.make_async_copy(enc_in, enc_keep, in_sems.at[2 * chunks]))
    ahead = 2
    for copy in loads[:ahead]:
        copy.start()
    stores = []
    for n, at in enumerate(spans):
        if n + ahead < len(loads):
            loads[n + ahead].start()
        loads[n].wait()
        stage[at] = scale * narrow[at].astype(F32)
        stores.append(pltpu.make_async_copy(stage.at[at], kgrad_out.at[at], out_sems.at[n]))
        stores[-1].start()
    loads[-1].wait()
    stores.append(pltpu.make_async_copy(enc_keep, enc_out, out_sems.at[2 * chunks]))
    stores[-1].start()
    wide = scale * small_in[...].astype(F32)
    obs_out[...] = wide[: obs_out.shape[0]]
    field_out[...] = wide[obs_out.shape[0] : obs_out.shape[0] + field_out.shape[0]]
    for copy in stores:
        copy.wait()


def per_device(
    grid_fields, obs_values, obs_count, obs_cell, obs_valid, obs_dist2,
    field_weight, obs_weight, conv_kernel, cotangent,
):
    rows, cols, channels = cotangent.shape
    lat_parts = lax.axis_size("lat")
    lon_parts = lax.axis_size("lon")
    parts = lat_parts * lon_parts
    fields = grid_fields.shape[0]
    width = obs_values.shape[3]
    capacity = obs_values.shape[2]
    wide = cols + SIDE
    tiles = TAPS * TAPS * channels // 16
    tiles = -(-tiles // parts) * parts
    plan = stage_plan(lat_parts, lon_parts, True)
    hops = sum(stage[1] - 1 for stage in plan)
    deep = -(-(width + fields) // 128) * 128
    small_rows = -(-(width + fields) // 16) * 16
    vmem = pl.BlockSpec(memory_space=pltpu.VMEM)
    anywhere = pl.BlockSpec(memory_space=pl.ANY)
    pads = [pltpu.VMEM((rows + 4, wide, channels), BF16)] * 4
    encoded, kgrad, small = pl.pallas_call(
        functools.partial(kernel, lat_parts, lon_parts),
        out_shape=(
            jax.ShapeDtypeStruct((rows, cols, channels), BF16),
            jax.ShapeDtypeStruct((2, tiles, 16, channels), BF16),
            jax.ShapeDtypeStruct((small_rows, channels), BF16),
        ),
        in_specs=[vmem, anywhere] + [vmem] * 6 + [anywhere] * 2,
        out_specs=(anywhere, anywhere, vmem),
        scratch_shapes=[
            pltpu.VMEM(conv_kernel.shape, BF16),
            pltpu.VMEM((rows, cols, channels), BF16),
            pltpu.VMEM((parts, 3, 128), F32),
            pltpu.VMEM((parts, capacity + 16, width), BF16),
            pltpu.VMEM((parts, capacity + 16, width), BF16),
            pltpu.VMEM((rows, cols, channels), BF16),
            pltpu.VMEM((deep, rows * cols), BF16),
            pltpu.VMEM((deep, channels), BF16),
            pltpu.VMEM((4, TAPS * channels, TAPS * channels), BF16),
            *pads,
            pltpu.VMEM((4, 4, SIDE, channels), BF16),
            pltpu.VMEM((4, 4, SIDE, channels), BF16),
            pltpu.VMEM((4, 2, 2, rows, channels), BF16),
            pltpu.VMEM((4, 2, 2, rows, channels), BF16),
            pltpu.VMEM((rows * SIDE, channels), F32),
            pltpu.VMEM((rows * SIDE, channels), F32),
            pltpu.VMEM((rows * SIDE, channels), F32),
            pltpu.VMEM((fields * rows, cols), F32),
            pltpu.VMEM((rows + 4, channels, cols), BF16),
            pltpu.VMEM((2, rows, cols, TAPS * channels), BF16),
            pltpu.VMEM((2, rows, SIDE, TAPS * channels), BF16),
            pltpu.VMEM((rows, cols, channels), F32),
            pltpu.VMEM((rows, cols, channels), F32),
            pltpu.VMEM((rows, cols, channels), F32),
            pltpu.VMEM((TAPS * channels, TAPS * channels), F32),
            pltpu.VMEM((2, tiles, 16, channels), BF16),
            pltpu.VMEM((2, tiles, 16, channels), BF16),
            pltpu.VMEM((2, tiles, 16, channels), BF16),
            pltpu.VMEM((len(plan) + 1, small_rows, channels), BF16),
            pltpu.VMEM((hops, small_rows, channels), BF16),
            pltpu.SemaphoreType.DMA((parts,)),
            pltpu.SemaphoreType.DMA((parts,)),
            pltpu.SemaphoreType.DMA((4,)),
            pltpu.SemaphoreType.DMA((5,)),
            pltpu.SemaphoreType.DMA((4, 8)),
            pltpu.SemaphoreType.DMA((4, 8)),
            pltpu.SemaphoreType.DMA((4, hops)),
            pltpu.SemaphoreType.DMA((4, hops)),
            pltpu.SemaphoreType.DMA((4, hops)),
            pltpu.SemaphoreType.DMA((4, hops)),
            pltpu.SemaphoreType.DMA((hops,)),
            pltpu.SemaphoreType.DMA((hops,)),
        ],
        compiler_params=pltpu.CompilerParams(
            collective_id=0, has_side_effects=True, vmem_limit_bytes=56 * 1024 * 1024
        ),
        name="encoder",
    )(
        grid_fields, obs_values, obs_count, jnp.swapaxes(obs_cell, 1, 2),
        jnp.swapaxes(obs_valid, 1, 2), jnp.swapaxes(obs_dist2, 1, 2),
        field_weight, obs_weight, conv_kernel, cotangent,
    )
    scale = 1.0 / (rows * lat_parts * cols * lon_parts) ** 0.5
    used = TAPS * TAPS * channels // 16
    chunks = math.gcd(used, 8)
    encoded, kernel_grad, obs_grad, field_grad = pl.pallas_call(
        functools.partial(widen, scale, chunks),
        in_specs=[anywhere] * 2 + [vmem],
        out_specs=[anywhere] * 2 + [vmem] * 2,
        out_shape=(
            jax.ShapeDtypeStruct((rows, cols, channels), BF16),
            jax.ShapeDtypeStruct((2, used, 16, channels), F32),
            jax.ShapeDtypeStruct((width, channels), F32),
            jax.ShapeDtypeStruct((fields, channels), F32),
        ),
        scratch_shapes=[
            pltpu.VMEM((2, used, 16, channels), BF16),
            pltpu.VMEM((2, used, 16, channels), F32),
            pltpu.VMEM((rows, cols, channels), BF16),
            pltpu.SemaphoreType.DMA((2 * chunks + 1,)),
            pltpu.SemaphoreType.DMA((2 * chunks + 1,)),
        ],
        compiler_params=pltpu.CompilerParams(vmem_limit_bytes=56 * 1024 * 1024),
        name="widen",
    )(encoded, kgrad, small)
    return encoded, kernel_grad.reshape(2, TAPS, TAPS, channels, channels), obs_grad, field_grad


def solution(mesh):
    return jax.shard_map(
        per_device,
        mesh=mesh,
        in_specs=(
            P(None, "lat", "lon"),
            P(("lat", "lon"), None, None, None),
            P(("lat", "lon"), None),
            P(("lat", "lon"), None, None),
            P(("lat", "lon"), None, None),
            P(("lat", "lon"), None, None),
            P(),
            P(),
            P(),
            P("lat", "lon", None),
        ),
        out_specs=(P("lat", "lon", None), P(), P(), P()),
        check_vma=False,
    )
```
